512 devices in a mesh: slab: 16 (over z), energy: 32 (over x, y, core).
Axes of the slice: x: 4, y: 4, z: 16, core: 2. Of those that a mesh axis runs over, the one named last changes fastest.
Arguments:
- green_left: bfloat16 [32, 32, 256, 512], P('energy', 'slab'), may hold values from -1.1 to 1.1
- sigma_lesser: bfloat16 [32, 32, 256, 512], P('energy', 'slab'), may hold values from -2.390625 to 2.390625
- coupling: float32 [32, 32], P('energy', 'slab'), may hold values from 0.56 to 0.99
- energy_weights: float32 [32], replicated, may hold values from 0.05 to 0.3
Outputs:
- lesser: float32 [32, 32, 256, 512], P(None, 'slab', 'energy')
- density: float32 [32, 256, 512], P('slab', 'energy')
The draws below stay inside these ranges and needn't reach their ends.
All inputs are finite; a program needn't handle non-finite values.
Results may differ from the reference program's by a relative error of at most 0.0003.
Values sent between devices are 32-bit elements; how exact they have to be, the bound alone decides.
No kernel may reach another device: no remote copies, remote signals or barrier semaphores. Data moves between devices by JAX's collectives and lax.ppermute only.
A program may use at most 64 MiB of HBM per device.

```python
import math
import jax
import jax.numpy as jnp
from jax import lax

NORB = 256
SAMPLE_LEVELS = 32
TOTAL_SLICES = 32


def draw_green_left(key, part):
    key = jax.random.fold_in(key, 11)
    random_modulus_draw, key_phase, key_noise = jax.random.split(key, 3)
    diag_shape = (SAMPLE_LEVELS, TOTAL_SLICES, NORB)
    full_shape = (SAMPLE_LEVELS, TOTAL_SLICES, NORB, 2 * NORB)
    magnitude = jnp.exp(jax.random.uniform(random_modulus_draw, diag_shape, jnp.float32, math.log(0.25), 0.0))
    noise = 0.12 * jnp.clip(jax.random.normal(key_noise, full_shape, jnp.float32), -1.7, 1.7)
    phase = jax.random.uniform(key_phase, diag_shape, jnp.float32, -math.pi + 0.2, -0.2)
    identity_block = jnp.eye(NORB, dtype=jnp.float32)
    diag_real = (magnitude * jnp.cos(phase))[..., None] * identity_block
    diag_imag = (magnitude * jnp.sin(phase))[..., None] * identity_block
    scaled = noise / math.sqrt(NORB)
    whole = jnp.concatenate([diag_real + scaled[..., :NORB], diag_imag + scaled[..., NORB:]], axis=-1)
    return whole.astype(jnp.bfloat16)


def draw_coupling(key, part):
    key = jax.random.fold_in(key, 23)
    key_offset_seed, random_cluster_state = jax.random.split(key, 2)
    starting_displacement = 0.99 - 0.04 * jax.random.uniform(key_offset_seed, (SAMPLE_LEVELS, TOTAL_SLICES), jnp.float32)
    parallel_cluster = jnp.where(jax.random.uniform(random_cluster_state, (SAMPLE_LEVELS, TOTAL_SLICES), jnp.float32) < 0.1, 0.6, 1.0)
    return (starting_displacement * parallel_cluster).astype(jnp.float32)


def steps_of(own_key, dims, pieces, low, high):
    loudness, own = 1.0, jax.random.fold_in(own_key, 6)
    for position, parts in pieces:
        draws = jnp.exp(jax.random.uniform(jax.random.fold_in(own, position), (parts,), jnp.float32, low / len(pieces), high / len(pieces)))
        loudness = loudness * jnp.repeat(draws, dims[position] // parts).reshape([-1 if axis == position else 1 for axis in range(len(dims))])
    return loudness


def bell_draw(rng, shape, width, limit, shards=(), held_as=jnp.bfloat16):
    values = width * jax.random.normal(rng, shape, jnp.float32)
    if shards:
        values = values * steps_of(rng, shape, shards, -0.22, 0.18)
    return jnp.clip(values, -limit, limit).astype(held_as)


def setup_inputs(seed: int = 0) -> dict:
    splits = jax.random.split(jax.random.key(seed), 5)
    green_left = draw_green_left(jax.random.fold_in(splits[4], 71), 0)
    sigma_lesser = bell_draw(splits[1], (SAMPLE_LEVELS, TOTAL_SLICES, NORB, 2 * NORB), 0.3, 2.390625, ((0, 32), (1, 16)))
    coupling = draw_coupling(jax.random.fold_in(splits[4], 71), 0)
    energy_weights = jnp.clip(jnp.exp(jax.random.uniform(splits[3], (SAMPLE_LEVELS,), jnp.float32, math.log(0.05), math.log(0.3))), 0.05, 0.3)
    return {"green_left": green_left, "sigma_lesser": sigma_lesser, "coupling": coupling, "energy_weights": energy_weights}


def complex_product(first_factor, second_factor):
    orbitals = first_factor.shape[-2]
    real_rows = jnp.einsum("...ij,...jk->...ik", first_factor[..., :orbitals], second_factor, precision=lax.Precision.HIGHEST)
    imag_rows = jnp.einsum("...ij,...jk->...ik", first_factor[..., orbitals:], second_factor, precision=lax.Precision.HIGHEST)
    return jnp.concatenate([real_rows[..., :orbitals] - imag_rows[..., orbitals:], real_rows[..., orbitals:] + imag_rows[..., :orbitals]], axis=-1)


def dagger(matrix):
    orbitals = matrix.shape[-2]
    return jnp.concatenate([jnp.swapaxes(matrix[..., :orbitals], -1, -2), -jnp.swapaxes(matrix[..., orbitals:], -1, -2)], axis=-1)


def congruence(green, middle):
    return complex_product(complex_product(green, middle), dagger(green))


def reference(green_left, sigma_lesser, coupling, energy_weights):
    green = green_left.astype(jnp.float32)
    sigma = sigma_lesser.astype(jnp.float32)
    squared = coupling * coupling
    identity_block = jnp.eye(NORB, dtype=jnp.float32)
    contact = jnp.concatenate([jnp.zeros_like(identity_block), identity_block], axis=-1)
    contact = jnp.broadcast_to(contact, (SAMPLE_LEVELS, NORB, 2 * NORB))

    def advance(state, inputs):
        block_green, block_sigma, block_squared = inputs
        source_lead = congruence(block_green, block_sigma)
        updated = source_lead + block_squared[:, None, None] * congruence(block_green, state)
        return updated, updated

    _, stacked = lax.scan(advance, contact, (jnp.moveaxis(green, 1, 0), jnp.moveaxis(sigma, 1, 0), squared.T))
    lesser = jnp.moveaxis(stacked, 0, 1)
    density = jnp.einsum("e,ebrc->brc", energy_weights, lesser, precision=lax.Precision.HIGHEST)
    return lesser, density
```

```python
import functools

import jax
import jax.numpy as jnp
from jax import lax
from jax.experimental import pallas as pl
from jax.experimental.pallas import tpu as pltpu
from jax.sharding import PartitionSpec as P

F32, BF16 = jnp.float32, jnp.bfloat16
GROUPS = (2, 3, 4, 3, 2, 2)
VMEM_BYTES = 40 * 1024 * 1024


def split(value):
    high = value.astype(BF16)
    return high, (value - high.astype(F32)).astype(BF16)


def dot(first, second):
    return jnp.dot(first, second, preferred_element_type=F32)


def expanded(matrix):
    half = matrix.shape[0]
    turned = jnp.concatenate([-matrix[:, half:], matrix[:, :half]], axis=1)
    return jnp.concatenate([matrix, turned], axis=0)


def dagger_form(matrix):
    half = matrix.shape[0]
    real, imag = matrix[:, :half].T, matrix[:, half:].T
    return jnp.concatenate(
        [jnp.concatenate([real, -imag], axis=1), jnp.concatenate([imag, real], axis=1)], axis=0
    )


def product_narrow(green, value):
    high, low = split(value)
    return dot(green, expanded(high)) + dot(green, expanded(low))


def product_wide(first_high, first_low, value):
    high, low = split(value)
    wide = expanded(high)
    return dot(first_high, wide) + dot(first_low, wide) + dot(first_high, expanded(low))


def right_narrow(value, form):
    high, low = split(value)
    return dot(high, form) + dot(low, form)


def right_wide(value, form_high, form_low):
    high, low = split(value)
    return dot(high, form_high) + dot(low, form_high) + dot(high, form_low)


def setup_kernel(
    position, coupling, green, sigma, local, first, joint, high, low, form_high, form_low, form_first
):
    half = green.shape[1]
    lead, follow = coupling[0, 0], coupling[0, 1]
    green_first, green_second = green[0], green[1]
    form = dagger_form(green_first)
    form_first[...] = form
    contact = jnp.where(position[0] == 0, lead * lead, 0.0)
    turned = jnp.concatenate(
        [-green_first[:, half:].astype(F32), green_first[:, :half].astype(F32)], axis=1
    )
    partial = dot(green_first, expanded(sigma[0])) + contact * turned
    first_block = right_narrow(partial, form)
    first[...] = first_block
    middle = sigma[1].astype(F32) + (follow * follow) * first_block
    local[...] = right_narrow(product_narrow(green_second, middle), dagger_form(green_second))
    whole = (lead * follow) * dot(green_second, expanded(green_first))
    joint[...] = whole
    part_high, part_low = split(whole)
    high[...], low[...] = part_high, part_low
    form_high[...], form_low[...] = dagger_form(part_high), dagger_form(part_low)


def hop_kernel(local, high, low, form_high, form_low, state, out):
    partial = product_wide(high[...], low[...], state[...])
    out[...] = local[...] + right_wide(partial, form_high[...], form_low[...])


def skip_kernel(high, low, form_high, form_low, left, right, out, state):
    value = left[...] + right[...]
    state[...] = value
    out[...] = right_wide(
        product_wide(high[...], low[...], value), form_high[...], form_low[...]
    )


def join_kernel(received, joint, whole, high, low, form_high, form_low):
    first_high, first_low = split(received[...])
    product = product_wide(first_high, first_low, joint[...])
    whole[...] = product
    part_high, part_low = split(product)
    high[...], low[...] = part_high, part_low
    form_high[...], form_low[...] = dagger_form(part_high), dagger_form(part_low)


def last_kernel(
    coupling, green, form_first, first, local, high, low, form_high, form_low, state, out
):
    rows = out.shape[2]
    lead = coupling[0, 0]
    value = state[...]
    block = first[...] + (lead * lead) * right_narrow(
        product_narrow(green[0], value), form_first[...]
    )
    out[:, 0] = block.reshape(-1, rows, block.shape[-1])
    block = local[...] + right_wide(
        product_wide(high[...], low[...], value), form_high[...], form_low[...]
    )
    out[:, 1] = block.reshape(-1, rows, block.shape[-1])


def density_kernel(weights, blocks, out):
    total = weights[0] * blocks[0]
    for level in range(1, blocks.shape[0]):
        total = total + weights[level] * blocks[level]
    out[...] = total


VMEM, SMEM = pl.BlockSpec(memory_space=pltpu.VMEM), pl.BlockSpec(memory_space=pltpu.SMEM)


def call(kernel, in_specs, shapes, flops):
    return pl.pallas_call(
        kernel,
        in_specs=in_specs,
        out_specs=jax.tree.map(lambda _: VMEM, shapes),
        out_shape=shapes,
        compiler_params=pltpu.CompilerParams(vmem_limit_bytes=VMEM_BYTES),
        cost_estimate=pl.CostEstimate(flops=flops, bytes_accessed=4 << 20, transcendentals=0),
    )


def plan(sizes):
    groups = len(sizes)
    heads = [sum(sizes[:k]) for k in range(groups)]
    tails = [head + size - 1 for head, size in zip(heads, sizes)]
    arrive = [0] + [sizes[0] + k - 1 for k in range(1, groups)]
    steps = {}

    def move(step, kind, source, target, role):
        steps.setdefault(step, []).append((kind, source, target, role))

    for k in range(groups):
        head, tail, size = heads[k], tails[k], sizes[k]
        middle = 0 < k < groups - 1
        if k == 0:
            for i in range(1, size):
                move(i, "forward", head + i - 1, head + i, "enter")
            move(size, "forward", tail, heads[1], "skip" if groups > 2 else "enter")
        if middle:
            for i in range(1, size):
                move(i, "forward", head + i - 1, head + i, "chain")
                move(i, "backward", tail - i + 1, tail - i, "join")
            own = "forward" if size < arrive[k] + 1 else "extra"
            move(size, own, tail, heads[k + 1], "hold")
            last = k + 1 == groups - 1
            move(arrive[k] + 1, "forward", head, heads[k + 1], "end" if last else "skip")
        if k > 0:
            delay = 1 if middle else 0
            for i in range(1, size):
                role = "enter" if head + i < tail else "keep"
                move(arrive[k] + delay + i, "forward", head + i - 1, head + i, role)
    return [steps[s] for s in sorted(steps)], heads


def member(position, places):
    mask = sum(1 << place for place in set(places))
    return ((jnp.int32(mask) >> position) & 1) == 1


def per_device(green_left, sigma_lesser, coupling, energy_weights):
    green, sigma = green_left[0], sigma_lesser[0]
    half, width = green.shape[1:]
    slabs, levels = lax.axis_size("slab"), lax.axis_size("energy")
    position = lax.axis_index("slab").astype(jnp.int32)
    wide = jax.ShapeDtypeStruct((half, width), F32)
    narrow = jax.ShapeDtypeStruct((half, width), BF16)
    form = jax.ShapeDtypeStruct((width, width), BF16)
    cost = 2 * half * width * width
    assert sum(GROUPS) == slabs

    local, first, joint, high, low, form_high, form_low, form_first = call(
        setup_kernel,
        [SMEM, SMEM, VMEM, VMEM],
        [wide, wide, wide, narrow, narrow, form, form, form],
        9 * cost,
    )(position[None], coupling, green, sigma)
    joint_forms = (high, low, form_high, form_low)
    hop = call(hop_kernel, [VMEM] * 6, wide, 6 * cost)
    skip = call(skip_kernel, [VMEM] * 6, [wide, wide], 6 * cost)
    join = call(join_kernel, [VMEM] * 2, [wide, narrow, narrow, form, form], 3 * cost)

    steps, heads = plan(GROUPS)
    zero = jnp.zeros((half, width), F32)
    outgoing, held, state = local, zero, zero
    whole, whole_forms = joint, joint_forms
    pending = []
    for moves in steps:
        received = {}
        by_kind = {}
        for kind, source, target, role in moves:
            by_kind.setdefault(kind, []).append((source, target, role))
        for kind in ("forward", "extra", "backward"):
            if kind in by_kind:
                pairs = [(source, target) for source, target, _ in by_kind[kind]]
                payload = whole if kind == "backward" else outgoing
                received[kind] = lax.ppermute(payload, "slab", pairs)
        places = {}
        for kind in by_kind:
            for _, target, role in by_kind[kind]:
                places.setdefault(role, []).append(target)
        if pending:
            outgoing = lax.cond(
                member(position, pending),
                lambda _, value: hop(local, *joint_forms, value),
                lambda old, _: old,
                outgoing,
                state,
            )
            pending = []
        if "join" in places:
            whole, *whole_forms = lax.cond(
                member(position, places["join"]),
                lambda value, *_: tuple(join(value, joint)),
                lambda _, *old: old,
                received["backward"],
                whole,
                *whole_forms,
            )
        for kind in by_kind:
            holders = [target for _, target, role in by_kind[kind] if role == "hold"]
            if holders:
                held = jnp.where(member(position, holders), received[kind], held)
        front = received["forward"]
        if "skip" in places:
            outgoing, state = lax.cond(
                member(position, places["skip"]),
                lambda value, kept, *_: tuple(skip(*whole_forms, value, kept)),
                lambda _, __, *old: old,
                front,
                held,
                outgoing,
                state,
            )
            pending = places["skip"]
        if "end" in places:
            outgoing, state = lax.cond(
                member(position, places["end"]),
                lambda value, kept, *_: (hop(local, *joint_forms, value + kept), value + kept),
                lambda _, __, *old: old,
                front,
                held,
                outgoing,
                state,
            )
        chained = places.get("chain", []) + places.get("enter", [])
        if chained:
            outgoing = lax.cond(
                member(position, chained),
                lambda value, _: hop(local, *joint_forms, value),
                lambda _, old: old,
                front,
                outgoing,
            )
        entered = places.get("enter", []) + places.get("keep", [])
        if entered:
            state = jnp.where(member(position, entered), front, state)

    rows = half // levels
    blocks = call(
        last_kernel,
        [SMEM] + [VMEM] * 9,
        jax.ShapeDtypeStruct((levels, 2, rows, width), F32),
        10 * cost,
    )(coupling, green, form_first, first, local, *joint_forms, state)
    block_rows = lax.all_to_all(blocks, "energy", split_axis=0, concat_axis=0, tiled=True)
    density = call(
        density_kernel,
        [SMEM, VMEM],
        jax.ShapeDtypeStruct((2, rows, width), F32),
        2 * half * width,
    )(energy_weights, block_rows)
    return block_rows, density


def solution(mesh):
    in_specs = (
        P("energy", "slab", None, None),
        P("energy", "slab", None, None),
        P("energy", "slab"),
        P(),
    )
    out_specs = (P(None, "slab", "energy", None), P("slab", "energy", None))
    return jax.shard_map(
        per_device, mesh=mesh, in_specs=in_specs, out_specs=out_specs, check_vma=False
    )
```

```python
import functools

import jax
import jax.numpy as jnp
from jax import lax
from jax.experimental import pallas as pl
from jax.experimental.pallas import tpu as pltpu
from jax.sharding import PartitionSpec as P

F32, BF16 = jnp.float32, jnp.bfloat16
GROUPS = (2, 3, 4, 3, 2, 2)
VMEM_BYTES = 40 * 1024 * 1024


def split(value):
    high = value.astype(BF16)
    return high, (value - high.astype(F32)).astype(BF16)


def dot(first, second):
    return jnp.dot(first, second, preferred_element_type=F32)


def expanded(matrix):
    half = matrix.shape[0]
    turned = jnp.concatenate([-matrix[:, half:], matrix[:, :half]], axis=1)
    return jnp.concatenate([matrix, turned], axis=0)


def dagger_form(matrix):
    half = matrix.shape[0]
    real, imag = matrix[:, :half].T, matrix[:, half:].T
    return jnp.concatenate(
        [jnp.concatenate([real, -imag], axis=1), jnp.concatenate([imag, real], axis=1)], axis=0
    )


def product_narrow(green, value):
    high, low = split(value)
    return dot(green, expanded(high)) + dot(green, expanded(low))


def product_wide(first_high, first_low, value):
    high, low = split(value)
    wide = expanded(high)
    return dot(first_high, wide) + dot(first_low, wide) + dot(first_high, expanded(low))


def right_narrow(value, form):
    high, low = split(value)
    return dot(high, form) + dot(low, form)


def right_wide(value, form_high, form_low):
    high, low = split(value)
    return dot(high, form_high) + dot(low, form_high) + dot(high, form_low)


def setup_kernel(
    position, coupling, green, sigma, local, first, joint, high, low, form_high, form_low, form_first
):
    half = green.shape[1]
    lead, follow = coupling[0, 0], coupling[0, 1]
    green_first, green_second = green[0], green[1]
    form = dagger_form(green_first)
    form_first[...] = form
    contact = jnp.where(position[0] == 0, lead * lead, 0.0)
    turned = jnp.concatenate(
        [-green_first[:, half:].astype(F32), green_first[:, :half].astype(F32)], axis=1
    )
    partial = dot(green_first, expanded(sigma[0])) + contact * turned
    first_block = right_narrow(partial, form)
    first[...] = first_block
    middle = sigma[1].astype(F32) + (follow * follow) * first_block
    local[...] = right_narrow(product_narrow(green_second, middle), dagger_form(green_second))
    whole = (lead * follow) * dot(green_second, expanded(green_first))
    joint[...] = whole
    part_high, part_low = split(whole)
    high[...], low[...] = part_high, part_low
    form_high[...], form_low[...] = dagger_form(part_high), dagger_form(part_low)


def sandwich(high, low, form_high, form_low, value):
    partial = product_wide(high[...], low[...], value)
    return right_wide(partial, form_high[...], form_low[...])


def takes_part(places):
    mask = sum(1 << place for place in set(places))
    position = lax.axis_index("slab").astype(jnp.int32)
    return ((jnp.int32(mask) >> position) & 1) == 1


def step_kernel(roles, names, *refs):
    ref = dict(zip(names, refs))
    forms = [ref.get(name) for name in ("high", "low", "form_high", "form_low")]
    whole_forms = [ref.get("whole_" + name) for name in ("high", "low", "form_high", "form_low")]

    def hold(source):
        def body():
            ref["held_out"][...] = ref[source][...]

        return body

    for source in ("front", "extra"):
        if roles.get("hold_" + source):
            pl.when(takes_part(roles["hold_" + source]))(hold(source))
    arriving = roles["enter"] + roles["keep"] + roles["lead"]
    if "state" not in ref:

        @pl.when(jnp.logical_not(takes_part(arriving)))
        def _():
            ref["state_out"][...] = jnp.zeros_like(ref["state_out"])

    if arriving:

        @pl.when(takes_part(arriving))
        def _():
            ref["state_out"][...] = ref["front"][...]

    joined = roles["skip"] + roles["end"]
    if joined:

        @pl.when(takes_part(joined))
        def _():
            ref["state_out"][...] = ref["front"][...] + ref["held_out"][...]

    onward = roles["enter"] + roles["end"]
    if onward:

        @pl.when(takes_part(onward))
        def _():
            ref["out"][...] = ref["local"][...] + sandwich(*forms, ref["state_out"][...])

    beyond = roles["skip"] + roles["lead"]
    if beyond:

        @pl.when(takes_part(beyond))
        def _():
            ref["out"][...] = sandwich(*whole_forms, ref["state_out"][...])


def after_kernel(places, local, high, low, form_high, form_low, state, out):
    @pl.when(takes_part(places))
    def _():
        out[...] = local[...] + sandwich(high, low, form_high, form_low, state[...])


def join_kernel(places, heads, received, joint, *rest):
    product, high, low, form_high, form_low = rest[-5:]

    @pl.when(takes_part(places))
    def _():
        first_high, first_low = split(received[...])
        product[...] = product_wide(first_high, first_low, joint[...])

    if heads:

        @pl.when(takes_part(heads))
        def _():
            part_high, part_low = split(product[...])
            high[...], low[...] = part_high, part_low
            form_high[...], form_low[...] = dagger_form(part_high), dagger_form(part_low)


def last_kernel(
    coupling, green, form_first, first, local, high, low, form_high, form_low, state, out
):
    rows = out.shape[2]
    lead = coupling[0, 0]
    value = state[...]
    block = first[...] + (lead * lead) * right_narrow(
        product_narrow(green[0], value), form_first[...]
    )
    out[:, 0] = block.reshape(-1, rows, block.shape[-1])
    block = local[...] + right_wide(
        product_wide(high[...], low[...], value), form_high[...], form_low[...]
    )
    out[:, 1] = block.reshape(-1, rows, block.shape[-1])


def density_kernel(weights, blocks, out):
    total = weights[0] * blocks[0]
    for level in range(1, blocks.shape[0]):
        total = total + weights[level] * blocks[level]
    out[...] = total


VMEM, SMEM = pl.BlockSpec(memory_space=pltpu.VMEM), pl.BlockSpec(memory_space=pltpu.SMEM)


def call(kernel, in_specs, shapes, flops, aliases=None):
    return pl.pallas_call(
        kernel,
        in_specs=in_specs,
        out_specs=jax.tree.map(lambda _: VMEM, shapes),
        out_shape=shapes,
        input_output_aliases=aliases or {},
        compiler_params=pltpu.CompilerParams(vmem_limit_bytes=VMEM_BYTES),
        cost_estimate=pl.CostEstimate(flops=flops, bytes_accessed=4 << 20, transcendentals=0),
    )


def plan(sizes):
    groups = len(sizes)
    heads = [sum(sizes[:k]) for k in range(groups)]
    tails = [head + size - 1 for head, size in zip(heads, sizes)]
    arrive = [0] + [sizes[0] + k - 1 for k in range(1, groups)]
    steps = {}

    def move(step, kind, source, target, role):
        steps.setdefault(step, []).append((kind, source, target, role))

    for k in range(groups):
        head, tail, size = heads[k], tails[k], sizes[k]
        middle = 0 < k < groups - 1
        if k == 0:
            for i in range(1, size):
                move(i, "forward", head + i - 1, head + i, "enter")
            move(size, "forward", tail, heads[1], "lead" if groups > 2 else "enter")
        if middle:
            for i in range(1, size):
                move(i, "forward", head + i - 1, head + i, "enter")
                move(i, "backward", tail - i + 1, tail - i, "join")
            own = "forward" if size < arrive[k] + 1 else "extra"
            move(size, own, tail, heads[k + 1], "hold")
            last = k + 1 == groups - 1
            move(arrive[k] + 1, "forward", head, heads[k + 1], "end" if last else "skip")
        if k > 0:
            delay = 1 if middle else 0
            for i in range(1, size):
                role = "enter" if head + i < tail else "keep"
                move(arrive[k] + delay + i, "forward", head + i - 1, head + i, role)
    return [steps[s] for s in sorted(steps)], heads


def per_device(green_left, sigma_lesser, coupling, energy_weights):
    green, sigma = green_left[0], sigma_lesser[0]
    half, width = green.shape[1:]
    slabs, levels = lax.axis_size("slab"), lax.axis_size("energy")
    position = lax.axis_index("slab").astype(jnp.int32)
    wide = jax.ShapeDtypeStruct((half, width), F32)
    narrow = jax.ShapeDtypeStruct((half, width), BF16)
    form = jax.ShapeDtypeStruct((width, width), BF16)
    cost = 2 * half * width * width
    assert sum(GROUPS) == slabs

    local, first, joint, high, low, form_high, form_low, form_first = call(
        setup_kernel,
        [SMEM, SMEM, VMEM, VMEM],
        [wide, wide, wide, narrow, narrow, form, form, form],
        9 * cost,
    )(position[None], coupling, green, sigma)
    joint_forms = (high, low, form_high, form_low)
    steps, heads = plan(GROUPS)
    shared = {"local": local, "high": high, "low": low, "form_high": form_high, "form_low": form_low}
    joint_forms = (high, low, form_high, form_low)
    outgoing, product, held, state, whole_forms, posted = local, joint, None, None, None, ()
    for moves in steps:
        by_kind = {}
        for kind, source, target, role in moves:
            by_kind.setdefault(kind, []).append((source, target, role))
        received = {
            kind: lax.ppermute(
                product if kind == "backward" else outgoing,
                "slab",
                [(source, target) for source, target, _ in by_kind[kind]],
            )
            for kind in ("forward", "extra", "backward")
            if kind in by_kind
        }
        after = None
        if posted:
            after = call(
                functools.partial(after_kernel, posted), [VMEM] * 6, wide, 6 * cost
            )(local, *joint_forms, state)

        if "backward" in received:
            places = [target for _, target, _ in by_kind["backward"]]
            ready = [place for place in places if place in heads]
            kept = tuple(whole_forms) if whole_forms else ()
            product, *whole_forms = call(
                functools.partial(join_kernel, places, ready),
                [VMEM] * (2 + len(kept)),
                [wide, narrow, narrow, form, form],
                3 * cost,
                {2 + i: 1 + i for i in range(len(kept))},
            )(received["backward"], joint, *kept)

        roles = {}
        for role in ("enter", "keep", "lead", "skip", "end"):
            roles[role] = [target for _, target, name in by_kind["forward"] if name == role]
        for source, kind in (("front", "forward"), ("extra", "extra")):
            roles["hold_" + source] = [
                target for _, target, name in by_kind.get(kind, []) if name == "hold"
            ]
        holding = bool(roles["hold_front"] or roles["hold_extra"])
        joining = bool(roles["skip"] or roles["end"])
        inputs = {"front": received["forward"]}
        if "extra" in received:
            inputs["extra"] = received["extra"]
        if roles["enter"] or roles["end"]:
            inputs.update(shared)
        beyond = roles["skip"] + roles["lead"]
        if beyond:
            for name, value in zip(("high", "low", "form_high", "form_low"), whole_forms):
                inputs["whole_" + name] = value
        outputs = ["out", "state_out"]
        aliases = {}
        if state is not None:
            aliases[len(inputs)] = 1
            inputs["state"] = state
        if holding or joining:
            if held is not None:
                aliases[len(inputs)] = 2
                inputs["held"] = held
            outputs.append("held_out")
        if after is not None:
            aliases[len(inputs)] = 0
            inputs["after"] = after
        results = call(
            functools.partial(step_kernel, roles, tuple(inputs) + tuple(outputs)),
            [VMEM] * len(inputs),
            [wide] * len(outputs),
            6 * cost,
            aliases,
        )(*inputs.values())
        outgoing, state = results[:2]
        if holding or joining:
            held = results[2]
        posted = [place for place in beyond if place + 1 not in heads]

    rows = half // levels
    blocks = call(
        last_kernel,
        [SMEM] + [VMEM] * 9,
        jax.ShapeDtypeStruct((levels, 2, rows, width), F32),
        10 * cost,
    )(coupling, green, form_first, first, local, *joint_forms, state)
    block_rows = lax.all_to_all(blocks, "energy", split_axis=0, concat_axis=0, tiled=True)
    density = call(
        density_kernel,
        [SMEM, VMEM],
        jax.ShapeDtypeStruct((2, rows, width), F32),
        2 * half * width,
    )(energy_weights, block_rows)
    return block_rows, density


def solution(mesh):
    in_specs = (
        P("energy", "slab", None, None),
        P("energy", "slab", None, None),
        P("energy", "slab"),
        P(),
    )
    out_specs = (P(None, "slab", "energy", None), P("slab", "energy", None))
    return jax.shard_map(
        per_device, mesh=mesh, in_specs=in_specs, out_specs=out_specs, check_vma=False
    )
```

```python
import functools

import jax
import jax.numpy as jnp
from jax import lax
from jax.experimental import pallas as pl
from jax.experimental.pallas import tpu as pltpu
from jax.sharding import PartitionSpec as P

F32, BF16 = jnp.float32, jnp.bfloat16
GROUPS = (2, 2, 3, 4, 3, 2)
VMEM_BYTES = 40 * 1024 * 1024


def split(value):
    high = value.astype(BF16)
    return high, (value - high.astype(F32)).astype(BF16)


def dot(first, second):
    return jnp.dot(first, second, preferred_element_type=F32)


def expanded(matrix):
    half = matrix.shape[0]
    turned = jnp.concatenate([-matrix[:, half:], matrix[:, :half]], axis=1)
    return jnp.concatenate([matrix, turned], axis=0)


def dagger_form(matrix):
    half = matrix.shape[0]
    real, imag = matrix[:, :half].T, matrix[:, half:].T
    return jnp.concatenate(
        [jnp.concatenate([real, -imag], axis=1), jnp.concatenate([imag, real], axis=1)], axis=0
    )


def product_narrow(green, value):
    high, low = split(value)
    return dot(green, expanded(high)) + dot(green, expanded(low))


def product_wide(first_high, first_low, value):
    high, low = split(value)
    wide = expanded(high)
    return dot(first_high, wide) + dot(first_low, wide) + dot(first_high, expanded(low))


def right_narrow(value, form):
    high, low = split(value)
    return dot(high, form) + dot(low, form)


def right_wide(value, form_high, form_low):
    high, low = split(value)
    return dot(high, form_high) + dot(low, form_high) + dot(high, form_low)


def setup_kernel(
    position, coupling, green, sigma, local, first, joint, high, low, form_high, form_low, form_first
):
    half = green.shape[1]
    lead, follow = coupling[0, 0], coupling[0, 1]
    green_first, green_second = green[0], green[1]
    form = dagger_form(green_first)
    form_first[...] = form
    contact = jnp.where(position[0] == 0, lead * lead, 0.0)
    turned = jnp.concatenate(
        [-green_first[:, half:].astype(F32), green_first[:, :half].astype(F32)], axis=1
    )
    partial = dot(green_first, expanded(sigma[0])) + contact * turned
    first_block = right_narrow(partial, form)
    first[...] = first_block
    middle = sigma[1].astype(F32) + (follow * follow) * first_block
    local[...] = right_narrow(product_narrow(green_second, middle), dagger_form(green_second))
    whole = (lead * follow) * dot(green_second, expanded(green_first))
    joint[...] = whole
    part_high, part_low = split(whole)
    high[...], low[...] = part_high, part_low
    form_high[...], form_low[...] = dagger_form(part_high), dagger_form(part_low)


def sandwich(high, low, form_high, form_low, value):
    partial = product_wide(high[...], low[...], value)
    return right_wide(partial, form_high[...], form_low[...])


def takes_part(places):
    mask = sum(1 << place for place in set(places))
    position = lax.axis_index("slab").astype(jnp.int32)
    return ((jnp.int32(mask) >> position) & 1) == 1


def step_kernel(roles, names, *refs):
    ref = dict(zip(names, refs))
    forms = [ref.get(name) for name in ("high", "low", "form_high", "form_low")]
    whole_forms = [ref.get("whole_" + name) for name in ("high", "low", "form_high", "form_low")]

    def hold(source):
        def body():
            ref["held_out"][...] = ref[source][...]

        return body

    for source in ("front", "extra"):
        if roles.get("hold_" + source):
            pl.when(takes_part(roles["hold_" + source]))(hold(source))
    arriving = roles["enter"] + roles["keep"] + roles["lead"]
    if "state" not in ref:

        @pl.when(jnp.logical_not(takes_part(arriving)))
        def _():
            ref["state_out"][...] = jnp.zeros_like(ref["state_out"])

    if arriving:

        @pl.when(takes_part(arriving))
        def _():
            ref["state_out"][...] = ref["front"][...]

    joined = roles["skip"] + roles["end"]
    if joined:

        @pl.when(takes_part(joined))
        def _():
            ref["state_out"][...] = ref["front"][...] + ref["held_out"][...]

    onward = roles["enter"] + roles["end"]
    if onward:

        @pl.when(takes_part(onward))
        def _():
            ref["out"][...] = ref["local"][...] + sandwich(*forms, ref["state_out"][...])

    beyond = roles["skip"] + roles["lead"]
    if beyond:

        @pl.when(takes_part(beyond))
        def _():
            ref["out"][...] = sandwich(*whole_forms, ref["state_out"][...])


def after_kernel(places, local, high, low, form_high, form_low, state, out):
    @pl.when(takes_part(places))
    def _():
        out[...] = local[...] + sandwich(high, low, form_high, form_low, state[...])


def join_kernel(places, heads, received, joint, product, *forms):
    @pl.when(takes_part(places))
    def _():
        first_high, first_low = split(received[...])
        product[...] = product_wide(first_high, first_low, joint[...])

    if heads:

        @pl.when(takes_part(heads))
        def _():
            high, low, form_high, form_low = forms
            part_high, part_low = split(product[...])
            high[...], low[...] = part_high, part_low
            form_high[...], form_low[...] = dagger_form(part_high), dagger_form(part_low)


def last_kernel(
    places, coupling, green, form_first, first, local, high, low, form_high, form_low, front,
    state_in, out, state
):
    arriving = takes_part(places)

    @pl.when(arriving)
    def _():
        state[...] = front[...]

    @pl.when(jnp.logical_not(arriving))
    def _():
        state[...] = state_in[...]

    rows = out.shape[2]
    lead = coupling[0, 0]
    value = state[...]
    block = first[...] + (lead * lead) * right_narrow(
        product_narrow(green[0], value), form_first[...]
    )
    out[:, 0] = block.reshape(-1, rows, block.shape[-1])
    block = local[...] + right_wide(
        product_wide(high[...], low[...], value), form_high[...], form_low[...]
    )
    out[:, 1] = block.reshape(-1, rows, block.shape[-1])


def density_kernel(weights, blocks, out, kept, done):
    copy = pltpu.make_async_copy(blocks, kept, done)
    copy.start()
    total = weights[0] * blocks[0]
    for level in range(1, blocks.shape[0]):
        total = total + weights[level] * blocks[level]
    out[...] = total
    copy.wait()


VMEM, SMEM = pl.BlockSpec(memory_space=pltpu.VMEM), pl.BlockSpec(memory_space=pltpu.SMEM)
ANY = pl.BlockSpec(memory_space=pl.ANY)


def call(kernel, in_specs, shapes, flops, aliases=None, scratch=()):
    return pl.pallas_call(
        kernel,
        in_specs=in_specs,
        out_specs=jax.tree.map(lambda _: VMEM, shapes),
        out_shape=shapes,
        input_output_aliases=aliases or {},
        scratch_shapes=scratch,
        compiler_params=pltpu.CompilerParams(vmem_limit_bytes=VMEM_BYTES),
        cost_estimate=pl.CostEstimate(flops=flops, bytes_accessed=4 << 20, transcendentals=0),
    )


def plan(sizes):
    groups = len(sizes)
    heads = [sum(sizes[:k]) for k in range(groups)]
    tails = [head + size - 1 for head, size in zip(heads, sizes)]
    arrive = [0] + [sizes[0] + k - 1 for k in range(1, groups)]
    steps = {}

    def move(step, kind, source, target, role):
        steps.setdefault(step, []).append((kind, source, target, role))

    for k in range(groups):
        head, tail, size = heads[k], tails[k], sizes[k]
        middle = 0 < k < groups - 1
        if k == 0:
            for i in range(1, size):
                move(i, "forward", head + i - 1, head + i, "enter")
            move(size, "forward", tail, heads[1], "lead" if groups > 2 else "enter")
        if middle:
            for i in range(1, size):
                move(i, "forward", head + i - 1, head + i, "enter")
                move(i, "backward", tail - i + 1, tail - i, "join")
            own = "forward" if size < arrive[k] + 1 else "extra"
            move(size, own, tail, heads[k + 1], "hold")
            last = k + 1 == groups - 1
            move(arrive[k] + 1, "forward", head, heads[k + 1], "end" if last else "skip")
        if k > 0:
            delay = 1 if middle else 0
            for i in range(1, size):
                role = "enter" if head + i < tail else "keep"
                move(arrive[k] + delay + i, "forward", head + i - 1, head + i, role)
    return [steps[s] for s in sorted(steps)], heads


def per_device(green_left, sigma_lesser, coupling, energy_weights):
    green, sigma = green_left[0], sigma_lesser[0]
    half, width = green.shape[1:]
    slabs, levels = lax.axis_size("slab"), lax.axis_size("energy")
    position = lax.axis_index("slab").astype(jnp.int32)
    wide = jax.ShapeDtypeStruct((half, width), F32)
    narrow = jax.ShapeDtypeStruct((half, width), BF16)
    form = jax.ShapeDtypeStruct((width, width), BF16)
    cost = 2 * half * width * width
    assert sum(GROUPS) == slabs

    local, first, joint, high, low, form_high, form_low, form_first = call(
        setup_kernel,
        [SMEM, SMEM, VMEM, VMEM],
        [wide, wide, wide, narrow, narrow, form, form, form],
        9 * cost,
    )(position[None], coupling, green, sigma)
    joint_forms = (high, low, form_high, form_low)
    steps, heads = plan(GROUPS)
    shared = {"local": local, "high": high, "low": low, "form_high": form_high, "form_low": form_low}
    joint_forms = (high, low, form_high, form_low)
    outgoing, product, held, state, whole_forms, posted = local, joint, None, None, {}, ()
    for moves in steps:
        by_kind = {}
        for kind, source, target, role in moves:
            by_kind.setdefault(kind, []).append((source, target, role))
        received = {
            kind: lax.ppermute(
                product if kind == "backward" else outgoing,
                "slab",
                [(source, target) for source, target, _ in by_kind[kind]],
            )
            for kind in ("forward", "extra", "backward")
            if kind in by_kind
        }
        after = None
        if posted:
            after = call(
                functools.partial(after_kernel, posted), [VMEM] * 6, wide, 6 * cost
            )(local, *joint_forms, state)

        if "backward" in received:
            places = [target for _, target, _ in by_kind["backward"]]
            ready = [place for place in places if place in heads]
            product, *forms = call(
                functools.partial(join_kernel, places, ready),
                [VMEM] * 2,
                [wide] + [narrow, narrow, form, form] * bool(ready),
                3 * cost,
            )(received["backward"], joint)
            whole_forms.update({place: forms for place in ready})

        roles = {}
        for role in ("enter", "keep", "lead", "skip", "end"):
            roles[role] = [target for _, target, name in by_kind["forward"] if name == role]
        for source, kind in (("front", "forward"), ("extra", "extra")):
            roles["hold_" + source] = [
                target for _, target, name in by_kind.get(kind, []) if name == "hold"
            ]
        if moves is steps[-1]:
            break
        holding = bool(roles["hold_front"] or roles["hold_extra"])
        joining = bool(roles["skip"] or roles["end"])
        inputs = {"front": received["forward"]}
        if "extra" in received:
            inputs["extra"] = received["extra"]
        if roles["enter"] or roles["end"]:
            inputs.update(shared)
        beyond = roles["skip"] + roles["lead"]
        if beyond:
            (place,) = beyond
            for name, value in zip(("high", "low", "form_high", "form_low"), whole_forms[place]):
                inputs["whole_" + name] = value
        outputs = ["out", "state_out"]
        aliases = {}
        if state is not None:
            aliases[len(inputs)] = 1
            inputs["state"] = state
        if holding or joining:
            if held is not None:
                aliases[len(inputs)] = 2
                inputs["held"] = held
            outputs.append("held_out")
        if after is not None:
            aliases[len(inputs)] = 0
            inputs["after"] = after
        results = call(
            functools.partial(step_kernel, roles, tuple(inputs) + tuple(outputs)),
            [VMEM] * len(inputs),
            [wide] * len(outputs),
            6 * cost,
            aliases,
        )(*inputs.values())
        outgoing, state = results[:2]
        if holding or joining:
            held = results[2]
        posted = [place for place in beyond if place + 1 not in heads]

    rows = half // levels
    blocks = call(
        functools.partial(last_kernel, roles["keep"]),
        [SMEM] + [VMEM] * 10,
        jax.ShapeDtypeStruct((levels, 2, rows, width), F32),
        10 * cost,
        scratch=[pltpu.VMEM((half, width), F32)],
    )(coupling, green, form_first, first, local, *joint_forms, received["forward"], state)
    block_rows = lax.all_to_all(blocks, "energy", split_axis=0, concat_axis=0, tiled=True)
    density, lesser = pl.pallas_call(
        density_kernel,
        in_specs=[SMEM, VMEM],
        out_specs=[VMEM, ANY],
        out_shape=[
            jax.ShapeDtypeStruct((2, rows, width), F32),
            jax.ShapeDtypeStruct(block_rows.shape, F32),
        ],
        scratch_shapes=[pltpu.SemaphoreType.DMA],
        compiler_params=pltpu.CompilerParams(vmem_limit_bytes=VMEM_BYTES),
    )(energy_weights, block_rows)
    return lesser, density


def solution(mesh):
    in_specs = (
        P("energy", "slab", None, None),
        P("energy", "slab", None, None),
        P("energy", "slab"),
        P(),
    )
    out_specs = (P(None, "slab", "energy", None), P("slab", "energy", None))
    return jax.shard_map(
        per_device, mesh=mesh, in_specs=in_specs, out_specs=out_specs, check_vma=False
    )
```

```python
import functools

import jax
import jax.numpy as jnp
from jax import lax
from jax.experimental import pallas as pl
from jax.experimental.pallas import tpu as pltpu
from jax.sharding import PartitionSpec as P

F32, BF16 = jnp.float32, jnp.bfloat16
GROUPS = (2, 2, 3, 4, 3, 2)
VMEM_BYTES = 40 * 1024 * 1024


def split(value):
    high = value.astype(BF16)
    return high, (value - high.astype(F32)).astype(BF16)


def dot(first, second):
    return jnp.dot(first, second, preferred_element_type=F32)


def expanded(matrix):
    half = matrix.shape[0]
    turned = jnp.concatenate([-matrix[:, half:], matrix[:, :half]], axis=1)
    return jnp.concatenate([matrix, turned], axis=0)


def dagger_form(matrix):
    half = matrix.shape[0]
    real, imag = matrix[:, :half].T, matrix[:, half:].T
    return jnp.concatenate(
        [jnp.concatenate([real, -imag], axis=1), jnp.concatenate([imag, real], axis=1)], axis=0
    )


def product_narrow(green, value):
    high, low = split(value)
    return dot(green, expanded(high)) + dot(green, expanded(low))


def product_wide(first_high, first_low, value):
    high, low = split(value)
    wide = expanded(high)
    return dot(first_high, wide) + dot(first_low, wide) + dot(first_high, expanded(low))


def right_narrow(value, form):
    high, low = split(value)
    return dot(high, form) + dot(low, form)


def right_wide(value, form_high, form_low):
    high, low = split(value)
    return dot(high, form_high) + dot(low, form_high) + dot(high, form_low)


def setup_kernel(
    position, coupling, green, sigma, local, first, joint, high, low, form_high, form_low, form_first
):
    half = green.shape[1]
    lead, follow = coupling[0, 0], coupling[0, 1]
    green_first, green_second = green[0], green[1]
    form = dagger_form(green_first)
    form_first[...] = form
    contact = jnp.where(position[0] == 0, lead * lead, 0.0)
    turned = jnp.concatenate(
        [-green_first[:, half:].astype(F32), green_first[:, :half].astype(F32)], axis=1
    )
    partial = dot(green_first, expanded(sigma[0])) + contact * turned
    first_block = right_narrow(partial, form)
    first[...] = first_block
    middle = sigma[1].astype(F32) + (follow * follow) * first_block
    local[...] = right_narrow(product_narrow(green_second, middle), dagger_form(green_second))
    whole = (lead * follow) * dot(green_second, expanded(green_first))
    joint[...] = whole
    part_high, part_low = split(whole)
    high[...], low[...] = part_high, part_low
    form_high[...], form_low[...] = dagger_form(part_high), dagger_form(part_low)


def sandwich(high, low, form_high, form_low, value):
    partial = product_wide(high[...], low[...], value)
    return right_wide(partial, form_high[...], form_low[...])


def takes_part(places):
    mask = sum(1 << place for place in set(places))
    position = lax.axis_index("slab").astype(jnp.int32)
    return ((jnp.int32(mask) >> position) & 1) == 1


def chain_kernel(places, local, high, low, form_high, form_low, front, out):
    @pl.when(takes_part(places))
    def _():
        out[...] = local[...] + sandwich(high, low, form_high, form_low, front[...])


def step_kernel(roles, names, *refs):
    ref = dict(zip(names, refs))
    forms = [ref.get(name) for name in ("high", "low", "form_high", "form_low")]
    whole_forms = [ref.get("whole_" + name) for name in ("high", "low", "form_high", "form_low")]
    front, state = ref["front"], ref["state_out"]
    if "state" not in ref:
        state[...] = jnp.zeros_like(state)
    arriving = roles["enter"] + roles["keep"] + roles["lead"]
    if arriving:

        @pl.when(takes_part(arriving))
        def _():
            state[...] = front[...]

    joined = roles["skip"] + roles["end"]
    if joined:

        @pl.when(takes_part(joined))
        def _():
            state[...] = front[...] + ref["held"][...]

    onward = roles["enter"] + roles["end"]
    if onward:

        @pl.when(takes_part(onward))
        def _():
            ref["out"][...] = ref["local"][...] + sandwich(*forms, state[...])

    beyond = roles["skip"] + roles["lead"]
    if beyond:

        @pl.when(takes_part(beyond))
        def _():
            ref["out"][...] = sandwich(*whole_forms, state[...])


def after_kernel(places, local, high, low, form_high, form_low, state, out):
    @pl.when(takes_part(places))
    def _():
        out[...] = local[...] + sandwich(high, low, form_high, form_low, state[...])


def join_kernel(places, heads, received, joint, product, *forms):
    @pl.when(takes_part(places))
    def _():
        first_high, first_low = split(received[...])
        product[...] = product_wide(first_high, first_low, joint[...])

    if heads:

        @pl.when(takes_part(heads))
        def _():
            high, low, form_high, form_low = forms
            part_high, part_low = split(product[...])
            high[...], low[...] = part_high, part_low
            form_high[...], form_low[...] = dagger_form(part_high), dagger_form(part_low)


def last_kernel(
    places, coupling, green, form_first, first, local, high, low, form_high, form_low, front,
    state_in, out, state
):
    arriving = takes_part(places)

    @pl.when(arriving)
    def _():
        state[...] = front[...]

    @pl.when(jnp.logical_not(arriving))
    def _():
        state[...] = state_in[...]

    rows = out.shape[2]
    lead = coupling[0, 0]
    value = state[...]
    block = first[...] + (lead * lead) * right_narrow(
        product_narrow(green[0], value), form_first[...]
    )
    out[:, 0] = block.reshape(-1, rows, block.shape[-1])
    block = local[...] + right_wide(
        product_wide(high[...], low[...], value), form_high[...], form_low[...]
    )
    out[:, 1] = block.reshape(-1, rows, block.shape[-1])


def density_kernel(weights, blocks, out, kept, done):
    copy = pltpu.make_async_copy(blocks, kept, done)
    copy.start()
    total = weights[0] * blocks[0]
    for level in range(1, blocks.shape[0]):
        total = total + weights[level] * blocks[level]
    out[...] = total
    copy.wait()


VMEM, SMEM = pl.BlockSpec(memory_space=pltpu.VMEM), pl.BlockSpec(memory_space=pltpu.SMEM)
ANY = pl.BlockSpec(memory_space=pl.ANY)


def call(kernel, in_specs, shapes, flops, aliases=None, scratch=()):
    return pl.pallas_call(
        kernel,
        in_specs=in_specs,
        out_specs=jax.tree.map(lambda _: VMEM, shapes),
        out_shape=shapes,
        input_output_aliases=aliases or {},
        scratch_shapes=scratch,
        compiler_params=pltpu.CompilerParams(vmem_limit_bytes=VMEM_BYTES),
        cost_estimate=pl.CostEstimate(flops=flops, bytes_accessed=4 << 20, transcendentals=0),
    )


ROLES = ("enter", "lead", "skip", "end", "keep", "after")


def plan(sizes):
    groups = len(sizes)
    heads = [sum(sizes[:k]) for k in range(groups)]
    tails = [head + size - 1 for head, size in zip(heads, sizes)]
    arrive = [0] + [sizes[0] + k - 1 for k in range(1, groups)]
    longest = max(sizes[1:-1])
    chains = [[] for _ in range(longest + 1)]
    products = [[] for _ in range(longest)]
    count = max(arrive[k] + (0 < k < groups - 1) + sizes[k] - 1 for k in range(groups))
    sweep = [[] for _ in range(count + 1)]
    roles = [{role: [] for role in ROLES} for _ in range(count + 2)]

    def move(step, source, target, role):
        sweep[step].append((source, target))
        roles[step][role].append(target)

    for k in range(groups):
        head, tail, size = heads[k], tails[k], sizes[k]
        if k == 0:
            for i in range(1, size):
                move(i, i - 1, i, "enter")
            move(size, tail, heads[1], "lead")
            continue
        middle = k < groups - 1
        if middle:
            assert 1 < size <= arrive[k]
            for i in range(1, size + 1):
                chains[i].append((head + i - 1, head + i))
            for i in range(1, size):
                products[i].append((tail - i + 1, tail - i))
            move(arrive[k] + 1, head, heads[k + 1], "skip" if k + 1 < groups - 1 else "end")
            roles[arrive[k] + 1]["after"].append(head)
        for i in range(1, size):
            role = "enter" if head + i < tail else "keep"
            move(arrive[k] + middle + i, head + i - 1, head + i, role)
    return heads, tails, chains, products, sweep, roles


def per_device(green_left, sigma_lesser, coupling, energy_weights):
    green, sigma = green_left[0], sigma_lesser[0]
    half, width = green.shape[1:]
    slabs, levels = lax.axis_size("slab"), lax.axis_size("energy")
    position = lax.axis_index("slab").astype(jnp.int32)
    wide = jax.ShapeDtypeStruct((half, width), F32)
    narrow = jax.ShapeDtypeStruct((half, width), BF16)
    form = jax.ShapeDtypeStruct((width, width), BF16)
    cost = 2 * half * width * width
    assert sum(GROUPS) == slabs

    local, first, joint, high, low, form_high, form_low, form_first = call(
        setup_kernel,
        [SMEM, SMEM, VMEM, VMEM],
        [wide, wide, wide, narrow, narrow, form, form, form],
        9 * cost,
    )(position[None], coupling, green, sigma)
    joint_forms = (high, low, form_high, form_low)
    heads, tails, chains, products, sweep, roles = plan(GROUPS)
    group_of = {head: k for k, head in enumerate(heads)}
    shared = {"local": local, "high": high, "low": low, "form_high": form_high, "form_low": form_low}
    joint_forms = (high, low, form_high, form_low)

    composites, part = {}, local
    whole_forms, product = {}, joint
    state, outgoing = None, local
    for step in range(1, len(sweep)):
        role = roles[step]
        front = lax.ppermute(outgoing, "slab", sweep[step])
        if step < len(chains):
            composites[step] = lax.ppermute(part, "slab", chains[step])
        if step < len(products):
            earlier = lax.ppermute(product, "slab", products[step])
        if role["after"]:
            after = call(functools.partial(after_kernel, role["after"]), [VMEM] * 6, wide, 6 * cost)(
                local, *joint_forms, state
            )
        if step == len(sweep) - 1:
            break
        if step < len(chains) - 1:
            places = [target for _, target in chains[step] if target not in heads]
            part = call(functools.partial(chain_kernel, places), [VMEM] * 6, wide, 6 * cost)(
                local, *joint_forms, composites[step]
            )
        if step < len(products):
            places = [target for _, target in products[step]]
            ready = [place for place in places if place in heads]
            product, *forms = call(
                functools.partial(join_kernel, places, ready),
                [VMEM] * 2,
                [wide] + [narrow, narrow, form, form] * bool(ready),
                3 * cost,
            )(earlier, joint)
            whole_forms.update({place: forms for place in ready})
        inputs = {"front": front}
        if role["enter"] or role["end"]:
            inputs.update(shared)
        for place in role["skip"] + role["lead"]:
            for name, value in zip(("high", "low", "form_high", "form_low"), whole_forms[place]):
                inputs["whole_" + name] = value
        for place in role["skip"] + role["end"]:
            inputs["held"] = composites[GROUPS[group_of[place] - 1]]
        aliases = {}
        if state is not None:
            aliases[len(inputs)] = 1
            inputs["state"] = state
        if role["after"]:
            aliases[len(inputs)] = 0
            inputs["after"] = after
        outgoing, state = call(
            functools.partial(step_kernel, role, tuple(inputs) + ("out", "state_out")),
            [VMEM] * len(inputs),
            [wide, wide],
            6 * cost,
            aliases,
        )(*inputs.values())

    rows = half // levels
    blocks = call(
        functools.partial(last_kernel, role["keep"]),
        [SMEM] + [VMEM] * 10,
        jax.ShapeDtypeStruct((levels, 2, rows, width), F32),
        10 * cost,
        scratch=[pltpu.VMEM((half, width), F32)],
    )(coupling, green, form_first, first, local, *joint_forms, front, state)
    block_rows = lax.all_to_all(blocks, "energy", split_axis=0, concat_axis=0, tiled=True)
    density, lesser = pl.pallas_call(
        density_kernel,
        in_specs=[SMEM, VMEM],
        out_specs=[VMEM, ANY],
        out_shape=[
            jax.ShapeDtypeStruct((2, rows, width), F32),
            jax.ShapeDtypeStruct(block_rows.shape, F32),
        ],
        scratch_shapes=[pltpu.SemaphoreType.DMA],
        compiler_params=pltpu.CompilerParams(vmem_limit_bytes=VMEM_BYTES),
    )(energy_weights, block_rows)
    return lesser, density


def solution(mesh):
    in_specs = (
        P("energy", "slab", None, None),
        P("energy", "slab", None, None),
        P("energy", "slab"),
        P(),
    )
    out_specs = (P(None, "slab", "energy", None), P("slab", "energy", None))
    return jax.shard_map(
        per_device, mesh=mesh, in_specs=in_specs, out_specs=out_specs, check_vma=False
    )
```

```python
import functools

import jax
import jax.numpy as jnp
from jax import lax
from jax.experimental import pallas as pl
from jax.experimental.pallas import tpu as pltpu
from jax.sharding import PartitionSpec as P

F32, BF16 = jnp.float32, jnp.bfloat16
GROUPS = (2, 2, 3, 4, 3, 2)
VMEM_BYTES = 40 * 1024 * 1024


def split(value):
    high = value.astype(BF16)
    return high, (value - high.astype(F32)).astype(BF16)


def dot(first, second):
    return jnp.dot(first, second, preferred_element_type=F32)


def expanded(matrix):
    half = matrix.shape[0]
    turned = jnp.concatenate([-matrix[:, half:], matrix[:, :half]], axis=1)
    return jnp.concatenate([matrix, turned], axis=0)


def dagger_form(matrix):
    half = matrix.shape[0]
    real, imag = matrix[:, :half].T, matrix[:, half:].T
    return jnp.concatenate(
        [jnp.concatenate([real, -imag], axis=1), jnp.concatenate([imag, real], axis=1)], axis=0
    )


def product_narrow(green, value):
    high, low = split(value)
    return dot(green, expanded(high)) + dot(green, expanded(low))


def product_wide(first_high, first_low, value):
    high, low = split(value)
    wide = expanded(high)
    return dot(first_high, wide) + dot(first_low, wide) + dot(first_high, expanded(low))


def right_narrow(value, form):
    high, low = split(value)
    return dot(high, form) + dot(low, form)


def right_wide(value, form_high, form_low):
    high, low = split(value)
    return dot(high, form_high) + dot(low, form_high) + dot(high, form_low)


def source_kernel(coupling, green, sigma, local, first, form_first):
    half = green.shape[1]
    lead, follow = coupling[0, 0], coupling[0, 1]
    green_first, green_second = green[0], green[1]
    form = dagger_form(green_first)
    form_first[...] = form
    contact = jnp.where(lax.axis_index("slab") == 0, lead * lead, 0.0)
    turned = jnp.concatenate(
        [-green_first[:, half:].astype(F32), green_first[:, :half].astype(F32)], axis=1
    )
    partial = dot(green_first, expanded(sigma[0])) + contact * turned
    first_block = right_narrow(partial, form)
    first[...] = first_block
    middle = sigma[1].astype(F32) + (follow * follow) * first_block
    local[...] = right_narrow(product_narrow(green_second, middle), dagger_form(green_second))


def joint_kernel(coupling, green, joint, high, low, form_high, form_low):
    whole = (coupling[0, 0] * coupling[0, 1]) * dot(green[1], expanded(green[0]))
    joint[...] = whole
    part_high, part_low = split(whole)
    high[...], low[...] = part_high, part_low
    form_high[...], form_low[...] = dagger_form(part_high), dagger_form(part_low)


def turn_kernel(token, value, out):
    del token

    @pl.when(lax.axis_index("energy") % 2 == 0)
    def _():
        out[...] = value[...]


def sandwich(high, low, form_high, form_low, value):
    partial = product_wide(high[...], low[...], value)
    return right_wide(partial, form_high[...], form_low[...])


def takes_part(places):
    mask = sum(1 << place for place in set(places))
    position = lax.axis_index("slab").astype(jnp.int32)
    return ((jnp.int32(mask) >> position) & 1) == 1


def chain_kernel(places, local, high, low, form_high, form_low, *rest):
    *arrived, out = rest
    for core, front in enumerate(arrived):
        mine = takes_part(places)
        if len(arrived) > 1:
            mine = mine & (lax.axis_index("energy") % 2 != core)

        @pl.when(mine)
        def _(front=front):
            out[...] = local[...] + sandwich(high, low, form_high, form_low, front[...])


def step_kernel(roles, names, *refs):
    ref = dict(zip(names, refs))
    forms = [ref.get(name) for name in ("high", "low", "form_high", "form_low")]
    whole_forms = [ref.get("whole_" + name) for name in ("high", "low", "form_high", "form_low")]
    front, state = ref["front"], ref["state_out"]
    if "state" not in ref:
        state[...] = jnp.zeros_like(state)
    arriving = roles["enter"] + roles["keep"] + roles["lead"]
    if arriving:
        late = False
        if "late" in ref:
            late = takes_part(arriving) & (lax.axis_index("energy") % 2 == 0)

            @pl.when(late)
            def _():
                state[...] = ref["late"][...]

        @pl.when(takes_part(arriving) & jnp.logical_not(late))
        def _():
            state[...] = front[...]

    joined = roles["skip"] + roles["end"]
    if joined:

        @pl.when(takes_part(joined))
        def _():
            state[...] = front[...] + ref["held"][...]

    onward = roles["enter"] + roles["end"]
    if onward:

        @pl.when(takes_part(onward))
        def _():
            ref["out"][...] = ref["local"][...] + sandwich(*forms, state[...])

    beyond = roles["skip"] + roles["lead"]
    if beyond:

        @pl.when(takes_part(beyond))
        def _():
            ref["out"][...] = sandwich(*whole_forms, state[...])


def after_kernel(places, local, high, low, form_high, form_low, state, out):
    @pl.when(takes_part(places))
    def _():
        out[...] = local[...] + sandwich(high, low, form_high, form_low, state[...])


def join_kernel(places, heads, received, joint, product, *forms):
    @pl.when(takes_part(places))
    def _():
        first_high, first_low = split(received[...])
        product[...] = product_wide(first_high, first_low, joint[...])

    if heads:

        @pl.when(takes_part(heads))
        def _():
            high, low, form_high, form_low = forms
            part_high, part_low = split(product[...])
            high[...], low[...] = part_high, part_low
            form_high[...], form_low[...] = dagger_form(part_high), dagger_form(part_low)


def last_kernel(
    places, coupling, green, form_first, first, local, high, low, form_high, form_low, front,
    state_in, out, state
):
    arriving = takes_part(places)

    @pl.when(arriving)
    def _():
        state[...] = front[...]

    @pl.when(jnp.logical_not(arriving))
    def _():
        state[...] = state_in[...]

    rows = out.shape[2]
    lead = coupling[0, 0]
    value = state[...]
    block = first[...] + (lead * lead) * right_narrow(
        product_narrow(green[0], value), form_first[...]
    )
    out[:, 0] = block.reshape(-1, rows, block.shape[-1])
    block = local[...] + right_wide(
        product_wide(high[...], low[...], value), form_high[...], form_low[...]
    )
    out[:, 1] = block.reshape(-1, rows, block.shape[-1])


def density_kernel(weights, blocks, out, kept, done):
    parts = done.shape[0]
    size = blocks.shape[0] // parts
    copies = [
        pltpu.make_async_copy(
            blocks.at[pl.ds(part * size, size)], kept.at[pl.ds(part * size, size)], done.at[part]
        )
        for part in range(parts)
    ]
    for copy in copies:
        copy.start()
    total = weights[0] * blocks[0]
    for level in range(1, blocks.shape[0]):
        total = total + weights[level] * blocks[level]
    out[...] = total
    for copy in copies:
        copy.wait()


VMEM, SMEM = pl.BlockSpec(memory_space=pltpu.VMEM), pl.BlockSpec(memory_space=pltpu.SMEM)
ANY = pl.BlockSpec(memory_space=pl.ANY)


def call(kernel, in_specs, shapes, flops, aliases=None, scratch=()):
    return pl.pallas_call(
        kernel,
        in_specs=in_specs,
        out_specs=jax.tree.map(lambda _: VMEM, shapes),
        out_shape=shapes,
        input_output_aliases=aliases or {},
        scratch_shapes=scratch,
        compiler_params=pltpu.CompilerParams(vmem_limit_bytes=VMEM_BYTES),
        cost_estimate=pl.CostEstimate(flops=flops, bytes_accessed=4 << 20, transcendentals=0),
    )


def of_cores(pairs, levels, core):
    return [
        (source * levels + level, target * levels + level)
        for source, target in pairs
        for level in range(core, levels, 2)
    ]


ROLES = ("enter", "lead", "skip", "end", "keep", "after")


def plan(sizes):
    groups = len(sizes)
    heads = [sum(sizes[:k]) for k in range(groups)]
    tails = [head + size - 1 for head, size in zip(heads, sizes)]
    arrive = [0] + [sizes[0] + k - 1 for k in range(1, groups)]
    longest = max(sizes[1:-1])
    chains = [[] for _ in range(longest + 1)]
    products = [[] for _ in range(longest)]
    count = max(arrive[k] + (0 < k < groups - 1) + sizes[k] - 1 for k in range(groups))
    sweep = [[] for _ in range(count + 1)]
    roles = [{role: [] for role in ROLES} for _ in range(count + 2)]

    def move(step, source, target, role):
        sweep[step].append((source, target))
        roles[step][role].append(target)

    for k in range(groups):
        head, tail, size = heads[k], tails[k], sizes[k]
        if k == 0:
            for i in range(1, size):
                move(i, i - 1, i, "enter")
            move(size, tail, heads[1], "lead")
            continue
        middle = k < groups - 1
        if middle:
            assert 1 < size <= arrive[k]
            for i in range(1, size + 1):
                chains[i].append((head + i - 1, head + i))
            for i in range(1, size):
                products[i].append((tail - i + 1, tail - i))
            move(arrive[k] + 1, head, heads[k + 1], "skip" if k + 1 < groups - 1 else "end")
            roles[arrive[k] + 1]["after"].append(head)
        for i in range(1, size):
            role = "enter" if head + i < tail else "keep"
            move(arrive[k] + middle + i, head + i - 1, head + i, role)
    return heads, tails, chains, products, sweep, roles


def per_device(green_left, sigma_lesser, coupling, energy_weights):
    green, sigma = green_left[0], sigma_lesser[0]
    half, width = green.shape[1:]
    slabs, levels = lax.axis_size("slab"), lax.axis_size("energy")
    wide = jax.ShapeDtypeStruct((half, width), F32)
    narrow = jax.ShapeDtypeStruct((half, width), BF16)
    form = jax.ShapeDtypeStruct((width, width), BF16)
    cost = 2 * half * width * width
    assert sum(GROUPS) == slabs

    local, first, form_first = call(
        source_kernel, [SMEM, VMEM, VMEM], [wide, wide, form], 8 * cost
    )(coupling, green, sigma)
    joint, high, low, form_high, form_low = call(
        joint_kernel, [SMEM, VMEM], [wide, narrow, narrow, form, form], cost
    )(coupling, green)
    heads, tails, chains, products, sweep, roles = plan(GROUPS)
    group_of = {head: k for k, head in enumerate(heads)}
    shared = {"local": local, "high": high, "low": low, "form_high": form_high, "form_low": form_low}
    joint_forms = (high, low, form_high, form_low)

    composites, part = {}, local
    whole_forms, product = {}, joint
    state, outgoing = None, local
    for step in range(1, len(sweep)):
        role = roles[step]
        if step == 1:
            pairs = sweep[1] + chains[1]
            front = lax.ppermute(local, ("slab", "energy"), of_cores(pairs, levels, 1))
            partner = [(slab, slab ^ 1) for slab in range(slabs)]
            token = lax.ppermute(coupling, ("slab", "energy"), of_cores(partner, levels, 0))
            turned = call(turn_kernel, [VMEM] * 2, wide, 0)(token, local)
            late = lax.ppermute(turned, ("slab", "energy"), of_cores(pairs, levels, 0))
        else:
            front = lax.ppermute(outgoing, "slab", sweep[step])
        if 1 < step < len(chains):
            composites[step] = lax.ppermute(part, "slab", chains[step])
        if step < len(products):
            earlier = lax.ppermute(product, "slab", products[step])
        if role["after"]:
            after = call(functools.partial(after_kernel, role["after"]), [VMEM] * 6, wide, 6 * cost)(
                local, *joint_forms, state
            )
        if step == len(sweep) - 1:
            break
        if step < len(chains) - 1:
            places = [target for _, target in chains[step] if target not in heads]
            arrived = [front, late] if step == 1 else [composites[step]]
            part = call(
                functools.partial(chain_kernel, places), [VMEM] * (5 + len(arrived)), wide, 6 * cost
            )(local, *joint_forms, *arrived)
        if step < len(products):
            places = [target for _, target in products[step]]
            ready = [place for place in places if place in heads]
            product, *forms = call(
                functools.partial(join_kernel, places, ready),
                [VMEM] * 2,
                [wide] + [narrow, narrow, form, form] * bool(ready),
                3 * cost,
            )(earlier, joint)
            whole_forms.update({place: forms for place in ready})
        inputs = {"front": front}
        if step == 1:
            inputs["late"] = late
        if role["enter"] or role["end"]:
            inputs.update(shared)
        for place in role["skip"] + role["lead"]:
            for name, value in zip(("high", "low", "form_high", "form_low"), whole_forms[place]):
                inputs["whole_" + name] = value
        for place in role["skip"] + role["end"]:
            inputs["held"] = composites[GROUPS[group_of[place] - 1]]
        aliases = {}
        if state is not None:
            aliases[len(inputs)] = 1
            inputs["state"] = state
        if role["after"]:
            aliases[len(inputs)] = 0
            inputs["after"] = after
        outgoing, state = call(
            functools.partial(step_kernel, role, tuple(inputs) + ("out", "state_out")),
            [VMEM] * len(inputs),
            [wide, wide],
            6 * cost,
            aliases,
        )(*inputs.values())

    rows = half // levels
    blocks = call(
        functools.partial(last_kernel, role["keep"]),
        [SMEM] + [VMEM] * 10,
        jax.ShapeDtypeStruct((levels, 2, rows, width), F32),
        10 * cost,
        scratch=[pltpu.VMEM((half, width), F32)],
    )(coupling, green, form_first, first, local, *joint_forms, front, state)
    block_rows = lax.all_to_all(blocks, "energy", split_axis=0, concat_axis=0, tiled=True)
    density, lesser = pl.pallas_call(
        density_kernel,
        in_specs=[SMEM, VMEM],
        out_specs=[VMEM, ANY],
        out_shape=[
            jax.ShapeDtypeStruct((2, rows, width), F32),
            jax.ShapeDtypeStruct(block_rows.shape, F32),
        ],
        scratch_shapes=[pltpu.SemaphoreType.DMA((min(8, levels),))],
        compiler_params=pltpu.CompilerParams(vmem_limit_bytes=VMEM_BYTES),
    )(energy_weights, block_rows)
    return lesser, density


def solution(mesh):
    in_specs = (
        P("energy", "slab", None, None),
        P("energy", "slab", None, None),
        P("energy", "slab"),
        P(),
    )
    out_specs = (P(None, "slab", "energy", None), P("slab", "energy", None))
    return jax.shard_map(
        per_device, mesh=mesh, in_specs=in_specs, out_specs=out_specs, check_vma=False
    )
```

```python
import functools

import jax
import jax.numpy as jnp
from jax import lax
from jax.experimental import pallas as pl
from jax.experimental.pallas import tpu as pltpu
from jax.sharding import PartitionSpec as P

F32, BF16 = jnp.float32, jnp.bfloat16
GROUPS = (2, 2, 3, 4, 3, 2)
VMEM_BYTES = 40 * 1024 * 1024


def split(value):
    high = value.astype(BF16)
    return high, (value - high.astype(F32)).astype(BF16)


def dot(first, second):
    return jnp.dot(first, second, preferred_element_type=F32)


def expanded(matrix):
    half = matrix.shape[0]
    turned = jnp.concatenate([-matrix[:, half:], matrix[:, :half]], axis=1)
    return jnp.concatenate([matrix, turned], axis=0)


def dagger_form(matrix):
    half = matrix.shape[0]
    real, imag = matrix[:, :half].T, matrix[:, half:].T
    return jnp.concatenate(
        [jnp.concatenate([real, -imag], axis=1), jnp.concatenate([imag, real], axis=1)], axis=0
    )


def product_narrow(green, value):
    high, low = split(value)
    return dot(green, expanded(high)) + dot(green, expanded(low))


def product_wide(first_high, first_low, value):
    high, low = split(value)
    wide = expanded(high)
    return dot(first_high, wide) + dot(first_low, wide) + dot(first_high, expanded(low))


def right_narrow(value, form):
    high, low = split(value)
    return dot(high, form) + dot(low, form)


def right_wide(value, form_high, form_low):
    high, low = split(value)
    return dot(high, form_high) + dot(low, form_high) + dot(high, form_low)


def source_kernel(coupling, green, sigma, local, first, form_first):
    half = green.shape[1]
    lead, follow = coupling[:, 0:1], coupling[:, 1:2]
    green_first, green_second = green[0], green[1]
    form = dagger_form(green_first)
    form_first[...] = form
    contact = (lead * lead) * (lax.axis_index("slab") == 0).astype(F32)
    turned = jnp.concatenate(
        [-green_first[:, half:].astype(F32), green_first[:, :half].astype(F32)], axis=1
    )
    partial = dot(green_first, expanded(sigma[0])) + contact * turned
    first_block = right_narrow(partial, form)
    first[...] = first_block
    middle = sigma[1].astype(F32) + (follow * follow) * first_block
    local[...] = right_narrow(product_narrow(green_second, middle), dagger_form(green_second))


def joint_kernel(coupling, green, joint, high, low, form_high, form_low):
    whole = (coupling[:, 0:1] * coupling[:, 1:2]) * dot(green[1], expanded(green[0]))
    joint[...] = whole
    part_high, part_low = split(whole)
    high[...], low[...] = part_high, part_low
    form_high[...], form_low[...] = dagger_form(part_high), dagger_form(part_low)


def turn_kernel(token, value, out):
    del token

    @pl.when(lax.axis_index("energy") % 2 == 0)
    def _():
        out[...] = value[...]


def sandwich(high, low, form_high, form_low, value):
    partial = product_wide(high[...], low[...], value)
    return right_wide(partial, form_high[...], form_low[...])


def takes_part(places):
    mask = sum(1 << place for place in set(places))
    position = lax.axis_index("slab").astype(jnp.int32)
    return ((jnp.int32(mask) >> position) & 1) == 1


def chain_kernel(places, local, high, low, form_high, form_low, *rest):
    *arrived, out = rest
    for core, front in enumerate(arrived):
        mine = takes_part(places)
        if len(arrived) > 1:
            mine = mine & (lax.axis_index("energy") % 2 != core)

        @pl.when(mine)
        def _(front=front):
            out[...] = local[...] + sandwich(high, low, form_high, form_low, front[...])


def step_kernel(roles, names, *refs):
    ref = dict(zip(names, refs))
    forms = [ref.get(name) for name in ("high", "low", "form_high", "form_low")]
    whole_forms = [ref.get("whole_" + name) for name in ("high", "low", "form_high", "form_low")]
    front, state = ref["front"], ref["state_out"]
    if "state" not in ref:
        state[...] = jnp.zeros_like(state)
    arriving = roles["enter"] + roles["keep"] + roles["lead"]
    if arriving:
        late = False
        if "late" in ref:
            late = takes_part(arriving) & (lax.axis_index("energy") % 2 == 0)

            @pl.when(late)
            def _():
                state[...] = ref["late"][...]

        @pl.when(takes_part(arriving) & jnp.logical_not(late))
        def _():
            state[...] = front[...]

    joined = roles["skip"] + roles["end"]
    if joined:

        @pl.when(takes_part(joined))
        def _():
            state[...] = front[...] + ref["held"][...]

    onward = roles["enter"] + roles["end"]
    if onward:

        @pl.when(takes_part(onward))
        def _():
            ref["out"][...] = ref["local"][...] + sandwich(*forms, state[...])

    beyond = roles["skip"] + roles["lead"]
    if beyond:

        @pl.when(takes_part(beyond))
        def _():
            ref["out"][...] = sandwich(*whole_forms, state[...])


def after_kernel(places, local, high, low, form_high, form_low, state, out):
    @pl.when(takes_part(places))
    def _():
        out[...] = local[...] + sandwich(high, low, form_high, form_low, state[...])


def join_kernel(places, heads, count, *refs):
    arrived, (joint, product, *forms) = refs[:count], refs[count:]
    for core, received in enumerate(arrived):
        mine = takes_part(places)
        if count > 1:
            mine = mine & (lax.axis_index("energy") % 2 != core)

        @pl.when(mine)
        def _(received=received):
            first_high, first_low = split(received[...])
            product[...] = product_wide(first_high, first_low, joint[...])

    if heads:

        @pl.when(takes_part(heads))
        def _():
            high, low, form_high, form_low = forms
            part_high, part_low = split(product[...])
            high[...], low[...] = part_high, part_low
            form_high[...], form_low[...] = dagger_form(part_high), dagger_form(part_low)


def last_kernel(
    places, coupling, green, form_first, first, local, high, low, form_high, form_low, front,
    state_in, out, state
):
    arriving = takes_part(places)

    @pl.when(arriving)
    def _():
        state[...] = front[...]

    @pl.when(jnp.logical_not(arriving))
    def _():
        state[...] = state_in[...]

    rows = out.shape[2]
    lead = coupling[:, 0:1]
    value = state[...]
    block = first[...] + (lead * lead) * right_narrow(
        product_narrow(green[0], value), form_first[...]
    )
    out[:, 0] = block.reshape(-1, rows, block.shape[-1])
    block = local[...] + right_wide(
        product_wide(high[...], low[...], value), form_high[...], form_low[...]
    )
    out[:, 1] = block.reshape(-1, rows, block.shape[-1])


def density_kernel(weights, blocks, out, kept, done):
    parts = done.shape[0]
    size = blocks.shape[0] // parts
    copies = [
        pltpu.make_async_copy(
            blocks.at[pl.ds(part * size, size)], kept.at[pl.ds(part * size, size)], done.at[part]
        )
        for part in range(parts)
    ]
    for copy in copies:
        copy.start()
    total = weights[0:1, 0:1] * blocks[0]
    for level in range(1, blocks.shape[0]):
        total = total + weights[level : level + 1, 0:1] * blocks[level]
    out[...] = total
    for copy in copies:
        copy.wait()


VMEM = pl.BlockSpec(memory_space=pltpu.VMEM)
ANY = pl.BlockSpec(memory_space=pl.ANY)


def call(kernel, in_specs, shapes, flops, aliases=None, scratch=()):
    return pl.pallas_call(
        kernel,
        in_specs=in_specs,
        out_specs=jax.tree.map(lambda _: VMEM, shapes),
        out_shape=shapes,
        input_output_aliases=aliases or {},
        scratch_shapes=scratch,
        compiler_params=pltpu.CompilerParams(vmem_limit_bytes=VMEM_BYTES),
        cost_estimate=pl.CostEstimate(flops=flops, bytes_accessed=4 << 20, transcendentals=0),
    )


def of_cores(pairs, levels, core):
    return [
        (source * levels + level, target * levels + level)
        for source, target in pairs
        for level in range(core, levels, 2)
    ]


ROLES = ("enter", "lead", "skip", "end", "keep", "after")


def plan(sizes):
    groups = len(sizes)
    heads = [sum(sizes[:k]) for k in range(groups)]
    tails = [head + size - 1 for head, size in zip(heads, sizes)]
    arrive = [0] + [sizes[0] + k - 1 for k in range(1, groups)]
    longest = max(sizes[1:-1])
    chains = [[] for _ in range(longest + 1)]
    products = [[] for _ in range(longest)]
    count = max(arrive[k] + (0 < k < groups - 1) + sizes[k] - 1 for k in range(groups))
    sweep = [[] for _ in range(count + 1)]
    roles = [{role: [] for role in ROLES} for _ in range(count + 2)]

    def move(step, source, target, role):
        sweep[step].append((source, target))
        roles[step][role].append(target)

    for k in range(groups):
        head, tail, size = heads[k], tails[k], sizes[k]
        if k == 0:
            for i in range(1, size):
                move(i, i - 1, i, "enter")
            move(size, tail, heads[1], "lead")
            continue
        middle = k < groups - 1
        if middle:
            assert 1 < size <= arrive[k]
            for i in range(1, size + 1):
                chains[i].append((head + i - 1, head + i))
            for i in range(1, size):
                products[i].append((tail - i + 1, tail - i))
            move(arrive[k] + 1, head, heads[k + 1], "skip" if k + 1 < groups - 1 else "end")
            roles[arrive[k] + 1]["after"].append(head)
        for i in range(1, size):
            role = "enter" if head + i < tail else "keep"
            move(arrive[k] + middle + i, head + i - 1, head + i, role)
    return heads, tails, chains, products, sweep, roles


def per_device(green_left, sigma_lesser, coupling, energy_weights):
    green, sigma = green_left[0], sigma_lesser[0]
    half, width = green.shape[1:]
    slabs, levels = lax.axis_size("slab"), lax.axis_size("energy")
    wide = jax.ShapeDtypeStruct((half, width), F32)
    narrow = jax.ShapeDtypeStruct((half, width), BF16)
    form = jax.ShapeDtypeStruct((width, width), BF16)
    cost = 2 * half * width * width
    assert sum(GROUPS) == slabs

    local, first, form_first = call(
        source_kernel, [VMEM, VMEM, VMEM], [wide, wide, form], 8 * cost
    )(coupling, green, sigma)
    joint, high, low, form_high, form_low = call(
        joint_kernel, [VMEM, VMEM], [wide, narrow, narrow, form, form], cost
    )(coupling, green)
    heads, tails, chains, products, sweep, roles = plan(GROUPS)
    group_of = {head: k for k, head in enumerate(heads)}
    shared = {"local": local, "high": high, "low": low, "form_high": form_high, "form_low": form_low}
    joint_forms = (high, low, form_high, form_low)

    composites, part = {}, local
    whole_forms, product = {}, joint
    state, outgoing = None, local
    for step in range(1, len(sweep)):
        role = roles[step]
        if step == 1:
            pairs = sweep[1] + chains[1]
            front = lax.ppermute(local, ("slab", "energy"), of_cores(pairs, levels, 1))
            partner = [(slab, slab ^ 1) for slab in range(slabs)]
            token = lax.ppermute(coupling, ("slab", "energy"), of_cores(partner, levels, 0))
            token = lax.ppermute(token, ("slab", "energy"), of_cores(partner, levels, 0))
            turned = call(turn_kernel, [VMEM] * 2, wide, 0)(token, local)
            late = lax.ppermute(turned, ("slab", "energy"), of_cores(pairs, levels, 0))
        else:
            front = lax.ppermute(outgoing, "slab", sweep[step])
        if 1 < step < len(chains):
            composites[step] = lax.ppermute(part, "slab", chains[step])
        if step == 1:
            pairs = products[1]
            earlier = lax.ppermute(product, ("slab", "energy"), of_cores(pairs, levels, 1))
            turned = call(turn_kernel, [VMEM] * 2, wide, 0)(token, product)
            later = lax.ppermute(turned, ("slab", "energy"), of_cores(pairs, levels, 0))
        elif step < len(products):
            earlier = lax.ppermute(product, "slab", products[step])
        if role["after"]:
            after = call(functools.partial(after_kernel, role["after"]), [VMEM] * 6, wide, 6 * cost)(
                local, *joint_forms, state
            )
        if step == len(sweep) - 1:
            break
        if step < len(chains) - 1:
            places = [target for _, target in chains[step] if target not in heads]
            arrived = [front, late] if step == 1 else [composites[step]]
            part = call(
                functools.partial(chain_kernel, places), [VMEM] * (5 + len(arrived)), wide, 6 * cost
            )(local, *joint_forms, *arrived)
        if step < len(products):
            places = [target for _, target in products[step]]
            ready = [place for place in places if place in heads]
            product, *forms = call(
                functools.partial(join_kernel, places, ready, 2 if step == 1 else 1),
                [VMEM] * (3 if step == 1 else 2),
                [wide] + [narrow, narrow, form, form] * bool(ready),
                3 * cost,
            )(*([earlier, later] if step == 1 else [earlier]), joint)
            whole_forms.update({place: forms for place in ready})
        inputs = {"front": front}
        if step == 1:
            inputs["late"] = late
        if role["enter"] or role["end"]:
            inputs.update(shared)
        for place in role["skip"] + role["lead"]:
            for name, value in zip(("high", "low", "form_high", "form_low"), whole_forms[place]):
                inputs["whole_" + name] = value
        for place in role["skip"] + role["end"]:
            inputs["held"] = composites[GROUPS[group_of[place] - 1]]
        aliases = {}
        if state is not None:
            aliases[len(inputs)] = 1
            inputs["state"] = state
        if role["after"]:
            aliases[len(inputs)] = 0
            inputs["after"] = after
        outgoing, state = call(
            functools.partial(step_kernel, role, tuple(inputs) + ("out", "state_out")),
            [VMEM] * len(inputs),
            [wide, wide],
            6 * cost,
            aliases,
        )(*inputs.values())

    weights = jnp.broadcast_to(energy_weights[:, None], (levels, 128))
    rows = half // levels
    blocks = call(
        functools.partial(last_kernel, role["keep"]),
        [VMEM] * 11,
        jax.ShapeDtypeStruct((levels, 2, rows, width), F32),
        10 * cost,
        scratch=[pltpu.VMEM((half, width), F32)],
    )(coupling, green, form_first, first, local, *joint_forms, front, state)
    block_rows = lax.all_to_all(blocks, "energy", split_axis=0, concat_axis=0, tiled=True)
    density, lesser = pl.pallas_call(
        density_kernel,
        in_specs=[VMEM, VMEM],
        out_specs=[VMEM, ANY],
        out_shape=[
            jax.ShapeDtypeStruct((2, rows, width), F32),
            jax.ShapeDtypeStruct(block_rows.shape, F32),
        ],
        scratch_shapes=[pltpu.SemaphoreType.DMA((min(8, levels),))],
        compiler_params=pltpu.CompilerParams(vmem_limit_bytes=VMEM_BYTES),
    )(weights, block_rows)
    return lesser, density


def solution(mesh):
    in_specs = (
        P("energy", "slab", None, None),
        P("energy", "slab", None, None),
        P("energy", "slab"),
        P(),
    )
    out_specs = (P(None, "slab", "energy", None), P("slab", "energy", None))
    return jax.shard_map(
        per_device, mesh=mesh, in_specs=in_specs, out_specs=out_specs, check_vma=False
    )
```

```python
import functools

import jax
import jax.numpy as jnp
from jax import lax
from jax.experimental import pallas as pl
from jax.experimental.pallas import tpu as pltpu
from jax.sharding import PartitionSpec as P

F32, BF16 = jnp.float32, jnp.bfloat16
GROUPS = (2, 2, 3, 4, 3, 2)
VMEM_BYTES = 40 * 1024 * 1024


def split(value):
    high = value.astype(BF16)
    return high, (value - high.astype(F32)).astype(BF16)


def dot(first, second):
    return jnp.dot(first, second, preferred_element_type=F32)


def expanded(matrix):
    half = matrix.shape[0]
    turned = jnp.concatenate([-matrix[:, half:], matrix[:, :half]], axis=1)
    return jnp.concatenate([matrix, turned], axis=0)


def dagger_form(matrix):
    half = matrix.shape[0]
    real, imag = matrix[:, :half].T, matrix[:, half:].T
    return jnp.concatenate(
        [jnp.concatenate([real, -imag], axis=1), jnp.concatenate([imag, real], axis=1)], axis=0
    )


def product_narrow(green, value):
    high, low = split(value)
    return dot(green, expanded(high)) + dot(green, expanded(low))


def product_wide(first_high, first_low, value):
    high, low = split(value)
    wide = expanded(high)
    return dot(first_high, wide) + dot(first_low, wide) + dot(first_high, expanded(low))


def right_narrow(value, form):
    high, low = split(value)
    return dot(high, form) + dot(low, form)


def right_wide(value, form_high, form_low):
    high, low = split(value)
    return dot(high, form_high) + dot(low, form_high) + dot(high, form_low)


def source_kernel(coupling, green, sigma, local, first, form_first):
    half = green.shape[1]
    lead, follow = coupling[:, 0:1], coupling[:, 1:2]
    green_first, green_second = green[0], green[1]
    form = dagger_form(green_first)
    form_first[...] = form
    contact = (lead * lead) * (lax.axis_index("slab") == 0).astype(F32)
    turned = jnp.concatenate(
        [-green_first[:, half:].astype(F32), green_first[:, :half].astype(F32)], axis=1
    )
    partial = dot(green_first, expanded(sigma[0])) + contact * turned
    first_block = right_narrow(partial, form)
    first[...] = first_block
    middle = sigma[1].astype(F32) + (follow * follow) * first_block
    local[...] = right_narrow(product_narrow(green_second, middle), dagger_form(green_second))


def joint_kernel(coupling, green, joint, high, low, form_high, form_low):
    whole = (coupling[:, 0:1] * coupling[:, 1:2]) * dot(green[1], expanded(green[0]))
    joint[...] = whole
    part_high, part_low = split(whole)
    high[...], low[...] = part_high, part_low
    form_high[...], form_low[...] = dagger_form(part_high), dagger_form(part_low)


def turn_kernel(token, value, out):
    del token

    @pl.when(lax.axis_index("energy") % 2 == 0)
    def _():
        out[...] = value[...]


def sandwich(high, low, form_high, form_low, value):
    partial = product_wide(high[...], low[...], value)
    return right_wide(partial, form_high[...], form_low[...])


def takes_part(places):
    mask = sum(1 << place for place in set(places))
    position = lax.axis_index("slab").astype(jnp.int32)
    return ((jnp.int32(mask) >> position) & 1) == 1


def chain_kernel(places, local, high, low, form_high, form_low, *rest):
    *arrived, out = rest
    for core, front in enumerate(arrived):
        mine = takes_part(places)
        if len(arrived) > 1:
            mine = mine & (lax.axis_index("energy") % 2 != core)

        @pl.when(mine)
        def _(front=front):
            out[...] = local[...] + sandwich(high, low, form_high, form_low, front[...])


def step_kernel(roles, names, *refs):
    ref = dict(zip(names, refs))
    forms = [ref.get(name) for name in ("high", "low", "form_high", "form_low")]
    whole_forms = [ref.get("whole_" + name) for name in ("high", "low", "form_high", "form_low")]
    front, state = ref["front"], ref["state_out"]
    if "state" not in ref:
        state[...] = jnp.zeros_like(state)
    arriving = roles["enter"] + roles["keep"] + roles["lead"]
    if arriving:
        late = False
        if "late" in ref:
            late = takes_part(arriving) & (lax.axis_index("energy") % 2 == 0)

            @pl.when(late)
            def _():
                state[...] = ref["late"][...]

        @pl.when(takes_part(arriving) & jnp.logical_not(late))
        def _():
            state[...] = front[...]

    joined = roles["skip"] + roles["end"]
    if joined:

        @pl.when(takes_part(joined))
        def _():
            state[...] = front[...] + ref["held"][...]

    if roles["beside"]:

        @pl.when(takes_part(roles["beside"]))
        def _():
            state[...] = ref["inner"][...]

    onward = roles["enter"] + roles["end"] + roles["beside"]
    if onward:

        @pl.when(takes_part(onward))
        def _():
            ref["out"][...] = ref["local"][...] + sandwich(*forms, state[...])

    beyond = roles["skip"] + roles["lead"]
    if beyond:

        @pl.when(takes_part(beyond))
        def _():
            ref["out"][...] = sandwich(*whole_forms, state[...])

    if roles["both"]:

        @pl.when(takes_part(roles["both"]))
        def _():
            ref["inner_out"][...] = ref["local"][...] + sandwich(*forms, state[...])


def after_kernel(places, local, high, low, form_high, form_low, state, out):
    @pl.when(takes_part(places))
    def _():
        out[...] = local[...] + sandwich(high, low, form_high, form_low, state[...])


def join_kernel(places, heads, count, *refs):
    arrived, (joint, product, *forms) = refs[:count], refs[count:]
    for core, received in enumerate(arrived):
        mine = takes_part(places)
        if count > 1:
            mine = mine & (lax.axis_index("energy") % 2 != core)

        @pl.when(mine)
        def _(received=received):
            first_high, first_low = split(received[...])
            product[...] = product_wide(first_high, first_low, joint[...])

    if heads:

        @pl.when(takes_part(heads))
        def _():
            high, low, form_high, form_low = forms
            part_high, part_low = split(product[...])
            high[...], low[...] = part_high, part_low
            form_high[...], form_low[...] = dagger_form(part_high), dagger_form(part_low)


def last_kernel(
    places, coupling, green, form_first, first, local, high, low, form_high, form_low, front,
    state_in, out, state
):
    arriving = takes_part(places)

    @pl.when(arriving)
    def _():
        state[...] = front[...]

    @pl.when(jnp.logical_not(arriving))
    def _():
        state[...] = state_in[...]

    rows = out.shape[2]
    lead = coupling[:, 0:1]
    value = state[...]
    block = first[...] + (lead * lead) * right_narrow(
        product_narrow(green[0], value), form_first[...]
    )
    out[:, 0] = block.reshape(-1, rows, block.shape[-1])
    block = local[...] + right_wide(
        product_wide(high[...], low[...], value), form_high[...], form_low[...]
    )
    out[:, 1] = block.reshape(-1, rows, block.shape[-1])


def density_kernel(weights, blocks, out, kept, done):
    parts = done.shape[0]
    size = blocks.shape[0] // parts
    copies = [
        pltpu.make_async_copy(
            blocks.at[pl.ds(part * size, size)], kept.at[pl.ds(part * size, size)], done.at[part]
        )
        for part in range(parts)
    ]
    for copy in copies:
        copy.start()
    total = weights[0:1, 0:1] * blocks[0]
    for level in range(1, blocks.shape[0]):
        total = total + weights[level : level + 1, 0:1] * blocks[level]
    out[...] = total
    for copy in copies:
        copy.wait()


VMEM = pl.BlockSpec(memory_space=pltpu.VMEM)
ANY = pl.BlockSpec(memory_space=pl.ANY)


def call(kernel, in_specs, shapes, flops, aliases=None, scratch=()):
    return pl.pallas_call(
        kernel,
        in_specs=in_specs,
        out_specs=jax.tree.map(lambda _: VMEM, shapes),
        out_shape=shapes,
        input_output_aliases=aliases or {},
        scratch_shapes=scratch,
        compiler_params=pltpu.CompilerParams(vmem_limit_bytes=VMEM_BYTES),
        cost_estimate=pl.CostEstimate(flops=flops, bytes_accessed=4 << 20, transcendentals=0),
    )


def of_cores(pairs, levels, core):
    return [
        (source * levels + level, target * levels + level)
        for source, target in pairs
        for level in range(core, levels, 2)
    ]


ROLES = ("enter", "lead", "skip", "end", "keep", "after", "both", "beside")


def plan(sizes):
    groups = len(sizes)
    heads = [sum(sizes[:k]) for k in range(groups)]
    tails = [head + size - 1 for head, size in zip(heads, sizes)]
    arrive = [0] + [sizes[0] + k - 1 for k in range(1, groups)]
    longest = max(sizes[1:-1])
    chains = [[] for _ in range(longest + 1)]
    products = [[] for _ in range(longest)]
    count = max(arrive[k] + (0 < k < groups - 1) + sizes[k] - 1 for k in range(groups))
    sweep = [[] for _ in range(count + 1)]
    roles = [{role: [] for role in ROLES} for _ in range(count + 2)]

    def move(step, source, target, role):
        sweep[step].append((source, target))
        roles[step][role].append(target)

    for k in range(groups):
        head, tail, size = heads[k], tails[k], sizes[k]
        if k == 0:
            for i in range(1, size):
                move(i, i - 1, i, "enter")
            move(size, tail, heads[1], "lead")
            continue
        middle = k < groups - 1
        if middle:
            assert 1 < size <= arrive[k]
            for i in range(1, size + 1):
                chains[i].append((head + i - 1, head + i))
            for i in range(1, size):
                products[i].append((tail - i + 1, tail - i))
            move(arrive[k] + 1, head, heads[k + 1], "skip" if k + 1 < groups - 1 else "end")
            if k == groups - 2 and size > 2:
                roles[arrive[k]]["both"].append(head)
            else:
                roles[arrive[k] + 1]["after"].append(head)
        together = k == groups - 2 and size > 2
        for i in range(1, size):
            if together and i == 1:
                roles[arrive[k] + 1]["beside"].append(head + 1)
                continue
            role = "enter" if head + i < tail else "keep"
            move(arrive[k] + (middle and not together) + i, head + i - 1, head + i, role)
    return heads, tails, chains, products, sweep, roles


def per_device(green_left, sigma_lesser, coupling, energy_weights):
    green, sigma = green_left[0], sigma_lesser[0]
    half, width = green.shape[1:]
    slabs, levels = lax.axis_size("slab"), lax.axis_size("energy")
    wide = jax.ShapeDtypeStruct((half, width), F32)
    narrow = jax.ShapeDtypeStruct((half, width), BF16)
    form = jax.ShapeDtypeStruct((width, width), BF16)
    cost = 2 * half * width * width
    assert sum(GROUPS) == slabs

    local, first, form_first = call(
        source_kernel, [VMEM, VMEM, VMEM], [wide, wide, form], 8 * cost
    )(coupling, green, sigma)
    joint, high, low, form_high, form_low = call(
        joint_kernel, [VMEM, VMEM], [wide, narrow, narrow, form, form], cost
    )(coupling, green)
    heads, tails, chains, products, sweep, roles = plan(GROUPS)
    group_of = {head: k for k, head in enumerate(heads)}
    shared = {"local": local, "high": high, "low": low, "form_high": form_high, "form_low": form_low}
    joint_forms = (high, low, form_high, form_low)

    composites, part = {}, local
    whole_forms, product = {}, joint
    state, outgoing = None, local
    for step in range(1, len(sweep)):
        role = roles[step]
        if step == 1:
            pairs = sweep[1] + chains[1]
            front = lax.ppermute(local, ("slab", "energy"), of_cores(pairs, levels, 1))
            partner = [(slab, slab ^ 1) for slab in range(slabs)]
            token = lax.ppermute(coupling, ("slab", "energy"), of_cores(partner, levels, 0))
            token = lax.ppermute(token, ("slab", "energy"), of_cores(partner, levels, 0))
            turned = call(turn_kernel, [VMEM] * 2, wide, 0)(token, local)
            late = lax.ppermute(turned, ("slab", "energy"), of_cores(pairs, levels, 0))
        else:
            front = lax.ppermute(outgoing, "slab", sweep[step])
        if 1 < step < len(chains):
            composites[step] = lax.ppermute(part, "slab", chains[step])
        if step == 1:
            pairs = products[1]
            earlier = lax.ppermute(product, ("slab", "energy"), of_cores(pairs, levels, 1))
            turned = call(turn_kernel, [VMEM] * 2, wide, 0)(token, product)
            later = lax.ppermute(turned, ("slab", "energy"), of_cores(pairs, levels, 0))
        elif step < len(products):
            earlier = lax.ppermute(product, "slab", products[step])
        if role["after"]:
            after = call(functools.partial(after_kernel, role["after"]), [VMEM] * 6, wide, 6 * cost)(
                local, *joint_forms, state
            )
        if step == len(sweep) - 1:
            break
        if step < len(chains) - 1:
            places = [target for _, target in chains[step] if target not in heads]
            arrived = [front, late] if step == 1 else [composites[step]]
            part = call(
                functools.partial(chain_kernel, places), [VMEM] * (5 + len(arrived)), wide, 6 * cost
            )(local, *joint_forms, *arrived)
        if step < len(products):
            places = [target for _, target in products[step]]
            ready = [place for place in places if place in heads]
            product, *forms = call(
                functools.partial(join_kernel, places, ready, 2 if step == 1 else 1),
                [VMEM] * (3 if step == 1 else 2),
                [wide] + [narrow, narrow, form, form] * bool(ready),
                3 * cost,
            )(*([earlier, later] if step == 1 else [earlier]), joint)
            whole_forms.update({place: forms for place in ready})
        inputs = {"front": front}
        if step == 1:
            inputs["late"] = late
        if role["beside"]:
            inputs["inner"] = inner
        if role["enter"] or role["end"] or role["both"] or role["beside"]:
            inputs.update(shared)
        for place in role["skip"] + role["lead"]:
            for name, value in zip(("high", "low", "form_high", "form_low"), whole_forms[place]):
                inputs["whole_" + name] = value
        for place in role["skip"] + role["end"]:
            inputs["held"] = composites[GROUPS[group_of[place] - 1]]
        aliases = {}
        if state is not None:
            aliases[len(inputs)] = 1
            inputs["state"] = state
        if role["after"]:
            aliases[len(inputs)] = 0
            inputs["after"] = after
        outputs = ("out", "state_out") + ("inner_out",) * bool(role["both"])
        outgoing, state, *inside = call(
            functools.partial(step_kernel, role, tuple(inputs) + outputs),
            [VMEM] * len(inputs),
            [wide] * len(outputs),
            6 * cost,
            aliases,
        )(*inputs.values())
        if role["both"]:
            (place,) = role["both"]
            inner = lax.ppermute(inside[0], "slab", [(place, place + 1)])

    weights = jnp.broadcast_to(energy_weights[:, None], (levels, 128))
    rows = half // levels
    blocks = call(
        functools.partial(last_kernel, role["keep"]),
        [VMEM] * 11,
        jax.ShapeDtypeStruct((levels, 2, rows, width), F32),
        10 * cost,
        scratch=[pltpu.VMEM((half, width), F32)],
    )(coupling, green, form_first, first, local, *joint_forms, front, state)
    block_rows = lax.all_to_all(blocks, "energy", split_axis=0, concat_axis=0, tiled=True)
    density, lesser = pl.pallas_call(
        density_kernel,
        in_specs=[VMEM, VMEM],
        out_specs=[VMEM, ANY],
        out_shape=[
            jax.ShapeDtypeStruct((2, rows, width), F32),
            jax.ShapeDtypeStruct(block_rows.shape, F32),
        ],
        scratch_shapes=[pltpu.SemaphoreType.DMA((min(8, levels),))],
        compiler_params=pltpu.CompilerParams(vmem_limit_bytes=VMEM_BYTES),
    )(weights, block_rows)
    return lesser, density


def solution(mesh):
    in_specs = (
        P("energy", "slab", None, None),
        P("energy", "slab", None, None),
        P("energy", "slab"),
        P(),
    )
    out_specs = (P(None, "slab", "energy", None), P("slab", "energy", None))
    return jax.shard_map(
        per_device, mesh=mesh, in_specs=in_specs, out_specs=out_specs, check_vma=False
    )
```

```python
import functools

import jax
import jax.numpy as jnp
from jax import lax
from jax.experimental import pallas as pl
from jax.experimental.pallas import tpu as pltpu
from jax.sharding import PartitionSpec as P

F32, BF16 = jnp.float32, jnp.bfloat16
GROUPS = (2, 2, 3, 4, 3, 2)
VMEM_BYTES = 40 * 1024 * 1024


def split(value):
    high = value.astype(BF16)
    return high, (value - high.astype(F32)).astype(BF16)


def dot(first, second):
    return jnp.dot(first, second, preferred_element_type=F32)


def expanded(matrix):
    half = matrix.shape[0]
    turned = jnp.concatenate([-matrix[:, half:], matrix[:, :half]], axis=1)
    return jnp.concatenate([matrix, turned], axis=0)


def dagger_form(matrix):
    half = matrix.shape[0]
    real, imag = matrix[:, :half].T, matrix[:, half:].T
    return jnp.concatenate(
        [jnp.concatenate([real, -imag], axis=1), jnp.concatenate([imag, real], axis=1)], axis=0
    )


def product_narrow(green, value):
    high, low = split(value)
    return dot(green, expanded(high)) + dot(green, expanded(low))


def product_wide(first_high, first_low, value):
    high, low = split(value)
    wide = expanded(high)
    return dot(first_high, wide) + dot(first_low, wide) + dot(first_high, expanded(low))


def right_narrow(value, form):
    high, low = split(value)
    return dot(high, form) + dot(low, form)


def right_wide(value, form_high, form_low):
    high, low = split(value)
    return dot(high, form_high) + dot(low, form_high) + dot(high, form_low)


def source_kernel(coupling, green, sigma, local, first, form_first):
    half = green.shape[1]
    lead, follow = coupling[:, 0:1], coupling[:, 1:2]
    green_first, green_second = green[0], green[1]
    form = dagger_form(green_first)
    form_first[...] = form
    contact = (lead * lead) * (lax.axis_index("slab") == 0).astype(F32)
    turned = jnp.concatenate(
        [-green_first[:, half:].astype(F32), green_first[:, :half].astype(F32)], axis=1
    )
    partial = dot(green_first, expanded(sigma[0])) + contact * turned
    first_block = right_narrow(partial, form)
    first[...] = first_block
    middle = sigma[1].astype(F32) + (follow * follow) * first_block
    local[...] = right_narrow(product_narrow(green_second, middle), dagger_form(green_second))


def joint_kernel(coupling, green, joint, high, low, form_high, form_low):
    whole = (coupling[:, 0:1] * coupling[:, 1:2]) * dot(green[1], expanded(green[0]))
    joint[...] = whole
    part_high, part_low = split(whole)
    high[...], low[...] = part_high, part_low
    form_high[...], form_low[...] = dagger_form(part_high), dagger_form(part_low)


def turn_kernel(token, value, out):
    del token

    @pl.when(lax.axis_index("energy") % 2 == 0)
    def _():
        out[...] = value[...]


def sandwich(high, low, form_high, form_low, value):
    partial = product_wide(high[...], low[...], value)
    return right_wide(partial, form_high[...], form_low[...])


def takes_part(places):
    mask = sum(1 << place for place in set(places))
    position = lax.axis_index("slab").astype(jnp.int32)
    return ((jnp.int32(mask) >> position) & 1) == 1


def chain_kernel(places, local, high, low, form_high, form_low, *rest):
    *arrived, out = rest
    for core, front in enumerate(arrived):
        mine = takes_part(places)
        if len(arrived) > 1:
            mine = mine & (lax.axis_index("energy") % 2 != core)

        @pl.when(mine)
        def _(front=front):
            out[...] = local[...] + sandwich(high, low, form_high, form_low, front[...])


def step_kernel(roles, names, *refs):
    ref = dict(zip(names, refs))
    forms = [ref.get(name) for name in ("high", "low", "form_high", "form_low")]
    whole_forms = [ref.get("whole_" + name) for name in ("high", "low", "form_high", "form_low")]
    front, state = ref["front"], ref["state_out"]
    if "state" not in ref:
        state[...] = jnp.zeros_like(state)
    arriving = roles["enter"] + roles["keep"] + roles["lead"]
    if arriving:
        late = False
        if "late" in ref:
            late = takes_part(arriving) & (lax.axis_index("energy") % 2 == 0)

            @pl.when(late)
            def _():
                state[...] = ref["late"][...]

        @pl.when(takes_part(arriving) & jnp.logical_not(late))
        def _():
            state[...] = front[...]

    joined = roles["skip"] + roles["end"]
    if joined:

        @pl.when(takes_part(joined))
        def _():
            state[...] = front[...] + ref["held"][...]

    if roles["beside"]:

        @pl.when(takes_part(roles["beside"]))
        def _():
            state[...] = ref["inner"][...]

    onward = roles["enter"] + roles["end"] + roles["beside"]
    if onward:

        @pl.when(takes_part(onward))
        def _():
            ref["out"][...] = ref["local"][...] + sandwich(*forms, state[...])

    beyond = roles["skip"] + roles["lead"]
    if beyond:

        @pl.when(takes_part(beyond))
        def _():
            ref["out"][...] = sandwich(*whole_forms, state[...])

    if roles["both"]:

        @pl.when(takes_part(roles["both"]))
        def _():
            ref["inner_out"][...] = ref["local"][...] + sandwich(*forms, state[...])


def after_kernel(places, local, high, low, form_high, form_low, state, out):
    @pl.when(takes_part(places))
    def _():
        out[...] = local[...] + sandwich(high, low, form_high, form_low, state[...])


def join_kernel(places, heads, count, *refs):
    arrived, (joint, product, *forms) = refs[:count], refs[count:]
    for core, received in enumerate(arrived):
        mine = takes_part(places)
        if count > 1:
            mine = mine & (lax.axis_index("energy") % 2 != core)

        @pl.when(mine)
        def _(received=received):
            first_high, first_low = split(received[...])
            product[...] = product_wide(first_high, first_low, joint[...])

    if heads:

        @pl.when(takes_part(heads))
        def _():
            high, low, form_high, form_low = forms
            part_high, part_low = split(product[...])
            high[...], low[...] = part_high, part_low
            form_high[...], form_low[...] = dagger_form(part_high), dagger_form(part_low)


def last_kernel(
    places, coupling, green, form_first, first, local, high, low, form_high, form_low, front,
    state_in, out, state
):
    arriving = takes_part(places)

    @pl.when(arriving)
    def _():
        state[...] = front[...]

    @pl.when(jnp.logical_not(arriving))
    def _():
        state[...] = state_in[...]

    rows = out.shape[2]
    lead = coupling[:, 0:1]
    value = state[...]
    half = value.shape[0]
    part_high, part_low = split(value)
    by_high = dot(jnp.concatenate([green[0], high[...], low[...]], axis=0), expanded(part_high))
    by_low = dot(jnp.concatenate([green[0], high[...]], axis=0), expanded(part_low))
    left_first = by_high[:half] + by_low[:half]
    left_joint = by_high[half : 2 * half] + by_high[2 * half :] + by_low[half:]
    block = first[...] + (lead * lead) * right_narrow(left_first, form_first[...])
    out[:, 0] = block.reshape(-1, rows, block.shape[-1])
    block = local[...] + right_wide(left_joint, form_high[...], form_low[...])
    out[:, 1] = block.reshape(-1, rows, block.shape[-1])


def density_kernel(weights, blocks, out, kept, done):
    parts = done.shape[0]
    size = blocks.shape[0] // parts
    copies = [
        pltpu.make_async_copy(
            blocks.at[pl.ds(part * size, size)], kept.at[pl.ds(part * size, size)], done.at[part]
        )
        for part in range(parts)
    ]
    for copy in copies:
        copy.start()
    total = weights[0:1, 0:1] * blocks[0]
    for level in range(1, blocks.shape[0]):
        total = total + weights[level : level + 1, 0:1] * blocks[level]
    out[...] = total
    for copy in copies:
        copy.wait()


VMEM = pl.BlockSpec(memory_space=pltpu.VMEM)
ANY = pl.BlockSpec(memory_space=pl.ANY)


def call(kernel, in_specs, shapes, flops, aliases=None, scratch=()):
    return pl.pallas_call(
        kernel,
        in_specs=in_specs,
        out_specs=jax.tree.map(lambda _: VMEM, shapes),
        out_shape=shapes,
        input_output_aliases=aliases or {},
        scratch_shapes=scratch,
        compiler_params=pltpu.CompilerParams(vmem_limit_bytes=VMEM_BYTES),
        cost_estimate=pl.CostEstimate(flops=flops, bytes_accessed=4 << 20, transcendentals=0),
    )


def of_cores(pairs, levels, core):
    return [
        (source * levels + level, target * levels + level)
        for source, target in pairs
        for level in range(core, levels, 2)
    ]


ROLES = ("enter", "lead", "skip", "end", "keep", "after", "both", "beside")


def plan(sizes):
    groups = len(sizes)
    heads = [sum(sizes[:k]) for k in range(groups)]
    tails = [head + size - 1 for head, size in zip(heads, sizes)]
    arrive = [0] + [sizes[0] + k - 1 for k in range(1, groups)]
    longest = max(sizes[1:-1])
    chains = [[] for _ in range(longest + 1)]
    products = [[] for _ in range(longest)]
    count = max(arrive[k] + (0 < k < groups - 1) + sizes[k] - 1 for k in range(groups))
    sweep = [[] for _ in range(count + 1)]
    roles = [{role: [] for role in ROLES} for _ in range(count + 2)]

    def move(step, source, target, role):
        sweep[step].append((source, target))
        roles[step][role].append(target)

    for k in range(groups):
        head, tail, size = heads[k], tails[k], sizes[k]
        if k == 0:
            for i in range(1, size):
                move(i, i - 1, i, "enter")
            move(size, tail, heads[1], "lead")
            continue
        middle = k < groups - 1
        if middle:
            assert 1 < size <= arrive[k]
            for i in range(1, size + 1):
                chains[i].append((head + i - 1, head + i))
            for i in range(1, size):
                products[i].append((tail - i + 1, tail - i))
            move(arrive[k] + 1, head, heads[k + 1], "skip" if k + 1 < groups - 1 else "end")
            if k == groups - 2 and size > 2:
                roles[arrive[k]]["both"].append(head)
            else:
                roles[arrive[k] + 1]["after"].append(head)
        together = k == groups - 2 and size > 2
        for i in range(1, size):
            if together and i == 1:
                roles[arrive[k] + 1]["beside"].append(head + 1)
                continue
            role = "enter" if head + i < tail else "keep"
            move(arrive[k] + (middle and not together) + i, head + i - 1, head + i, role)
    return heads, tails, chains, products, sweep, roles


def per_device(green_left, sigma_lesser, coupling, energy_weights):
    green, sigma = green_left[0], sigma_lesser[0]
    half, width = green.shape[1:]
    slabs, levels = lax.axis_size("slab"), lax.axis_size("energy")
    wide = jax.ShapeDtypeStruct((half, width), F32)
    narrow = jax.ShapeDtypeStruct((half, width), BF16)
    form = jax.ShapeDtypeStruct((width, width), BF16)
    cost = 2 * half * width * width
    assert sum(GROUPS) == slabs

    local, first, form_first = call(
        source_kernel, [VMEM, VMEM, VMEM], [wide, wide, form], 8 * cost
    )(coupling, green, sigma)
    joint, high, low, form_high, form_low = call(
        joint_kernel, [VMEM, VMEM], [wide, narrow, narrow, form, form], cost
    )(coupling, green)
    heads, tails, chains, products, sweep, roles = plan(GROUPS)
    group_of = {head: k for k, head in enumerate(heads)}
    shared = {"local": local, "high": high, "low": low, "form_high": form_high, "form_low": form_low}
    joint_forms = (high, low, form_high, form_low)

    composites, part = {}, local
    whole_forms, product = {}, joint
    state, outgoing = None, local
    for step in range(1, len(sweep)):
        role = roles[step]
        if step == 1:
            pairs = sweep[1] + chains[1]
            front = lax.ppermute(local, ("slab", "energy"), of_cores(pairs, levels, 1))
            partner = [(slab, slab ^ 1) for slab in range(slabs)]
            token = lax.ppermute(coupling, ("slab", "energy"), of_cores(partner, levels, 0))
            token = lax.ppermute(token, ("slab", "energy"), of_cores(partner, levels, 0))
            turned = call(turn_kernel, [VMEM] * 2, wide, 0)(token, local)
            late = lax.ppermute(turned, ("slab", "energy"), of_cores(pairs, levels, 0))
        else:
            front = lax.ppermute(outgoing, "slab", sweep[step])
        if 1 < step < len(chains):
            composites[step] = lax.ppermute(part, "slab", chains[step])
        if step == 1:
            pairs = products[1]
            earlier = lax.ppermute(product, ("slab", "energy"), of_cores(pairs, levels, 1))
            turned = call(turn_kernel, [VMEM] * 2, wide, 0)(token, product)
            later = lax.ppermute(turned, ("slab", "energy"), of_cores(pairs, levels, 0))
        elif step < len(products):
            earlier = lax.ppermute(product, "slab", products[step])
        if role["after"]:
            after = call(functools.partial(after_kernel, role["after"]), [VMEM] * 6, wide, 6 * cost)(
                local, *joint_forms, state
            )
        if step == len(sweep) - 1:
            break
        if step < len(chains) - 1:
            places = [target for _, target in chains[step] if target not in heads]
            arrived = [front, late] if step == 1 else [composites[step]]
            part = call(
                functools.partial(chain_kernel, places), [VMEM] * (5 + len(arrived)), wide, 6 * cost
            )(local, *joint_forms, *arrived)
        if step < len(products):
            places = [target for _, target in products[step]]
            ready = [place for place in places if place in heads]
            product, *forms = call(
                functools.partial(join_kernel, places, ready, 2 if step == 1 else 1),
                [VMEM] * (3 if step == 1 else 2),
                [wide] + [narrow, narrow, form, form] * bool(ready),
                3 * cost,
            )(*([earlier, later] if step == 1 else [earlier]), joint)
            whole_forms.update({place: forms for place in ready})
        inputs = {"front": front}
        if step == 1:
            inputs["late"] = late
        if role["beside"]:
            inputs["inner"] = inner
        if role["enter"] or role["end"] or role["both"] or role["beside"]:
            inputs.update(shared)
        for place in role["skip"] + role["lead"]:
            for name, value in zip(("high", "low", "form_high", "form_low"), whole_forms[place]):
                inputs["whole_" + name] = value
        for place in role["skip"] + role["end"]:
            inputs["held"] = composites[GROUPS[group_of[place] - 1]]
        aliases = {}
        if state is not None:
            aliases[len(inputs)] = 1
            inputs["state"] = state
        if role["after"]:
            aliases[len(inputs)] = 0
            inputs["after"] = after
        outputs = ("out", "state_out") + ("inner_out",) * bool(role["both"])
        outgoing, state, *inside = call(
            functools.partial(step_kernel, role, tuple(inputs) + outputs),
            [VMEM] * len(inputs),
            [wide] * len(outputs),
            6 * cost,
            aliases,
        )(*inputs.values())
        if role["both"]:
            (place,) = role["both"]
            inner = lax.ppermute(inside[0], "slab", [(place, place + 1)])

    weights = jnp.broadcast_to(energy_weights[:, None], (levels, 128))
    rows = half // levels
    blocks = call(
        functools.partial(last_kernel, role["keep"]),
        [VMEM] * 11,
        jax.ShapeDtypeStruct((levels, 2, rows, width), F32),
        10 * cost,
        scratch=[pltpu.VMEM((half, width), F32)],
    )(coupling, green, form_first, first, local, *joint_forms, front, state)
    block_rows = lax.all_to_all(blocks, "energy", split_axis=0, concat_axis=0, tiled=True)
    density, lesser = pl.pallas_call(
        density_kernel,
        in_specs=[VMEM, VMEM],
        out_specs=[VMEM, ANY],
        out_shape=[
            jax.ShapeDtypeStruct((2, rows, width), F32),
            jax.ShapeDtypeStruct(block_rows.shape, F32),
        ],
        scratch_shapes=[pltpu.SemaphoreType.DMA((min(8, levels),))],
        compiler_params=pltpu.CompilerParams(vmem_limit_bytes=VMEM_BYTES),
    )(weights, block_rows)
    return lesser, density


def solution(mesh):
    in_specs = (
        P("energy", "slab", None, None),
        P("energy", "slab", None, None),
        P("energy", "slab"),
        P(),
    )
    out_specs = (P(None, "slab", "energy", None), P("slab", "energy", None))
    return jax.shard_map(
        per_device, mesh=mesh, in_specs=in_specs, out_specs=out_specs, check_vma=False
    )
```
